32 devices in a mesh: groups: 2 (over x), img: 16 (over z, y, core).
Axes of the slice: x: 2, y: 2, z: 4, core: 2. Of those that a mesh axis runs over, the one named last changes fastest.
Arguments:
- tokens: bfloat16 [256, 196, 768], P(('groups', 'img')), parts along dimension 0, may hold values from -60 to 60
- pair_list: int32 [256, 2], P(('groups', 'img')), parts along dimension 0, may hold values from 0 to 127, as said below
- w_query: bfloat16 [768, 768], replicated, may hold values from -1.5 to 1.5
- w_key: bfloat16 [768, 768], replicated, may hold values from -1.5 to 1.5
- w_value: bfloat16 [768, 768], replicated, may hold values from -0.21875 to 0.21875
- w_out: bfloat16 [768, 768], replicated, may hold values from -0.21875 to 0.21875
- gain_query: float32 [768], replicated, may hold values from 0.1 to 1.9
- context_norm_gain: float32 [768], replicated, may hold values from 0.1 to 1.9
- conf_weight: float32 [768], replicated, may hold values from -0.21875 to 0.21875
Outputs:
- merged: float32 [256, 196, 768], P(('groups', 'img')), parts along dimension 0
The draws below stay inside these ranges and needn't reach their ends.
There are 2 independent parts, one for each index of `groups`. The reference program is written for one: setup_inputs(seed, part) draws one part's arguments, and reference() takes and returns one part's arrays. A program takes and returns all parts, laid end to end along the dimension named above; an argument that names none is the same for every part. Nothing has to cross between parts.
Inputs may be any that keep to these rules, and one draw needn't show every extreme that they name: Image i is held by device i // 8 of img, and row r of pair_list is listed at device r // 8, which holds the pair's first image. The second image differs from the first. Among the 8 rows of one device at most 1 name a second image held by any one device, and in every draw some device holds the second images of exactly 1 row of every device.
All inputs are finite; a program needn't handle non-finite values.
Results may differ from the reference program's by a relative error of at most 0.0009.
Values may be sent and summed in bfloat16 or wider, within the bound.
No kernel may reach another device: no remote copies, remote signals or barrier semaphores. Data moves between devices by JAX's collectives and lax.ppermute only.
A program may use at most 192 MiB of HBM per device.

```python
import math
import jax
import jax.numpy as jnp
from jax import lax

D = 768
HEADS = 12
L = 196
IMG_DEV = 8
SLOT = 1
PAIR_DEV = 8
IMGS = 128
PAIRS = 128
N_IMG = 16


def draw_tokens(key, part):
    key_list = jax.random.split(key, 4)
    col_scale = jnp.exp(jax.random.uniform(key_list[0], (D,), jnp.float32, math.log(0.3), math.log(3.0)))
    col_mean = jax.random.normal(key_list[1], (D,), jnp.float32) * 0.5
    row_scale = jnp.exp(jax.random.uniform(key_list[2], (IMGS, L, 1), jnp.float32, math.log(0.3), math.log(3.0)))
    base_draw = jax.random.normal(key_list[3], (IMGS, L, D), jnp.float32)
    values = (base_draw * row_scale + col_mean) * col_scale
    return jnp.clip(values, -60.0, 60.0).astype(jnp.bfloat16)


def weight_common(key, which_one):
    own_part = jnp.clip(jax.random.normal(jax.random.fold_in(key, 20 + which_one), (D, D), jnp.float32), -6.0, 6.0)
    values = own_part * D ** (-0.5)
    return jnp.clip(values, -1.5, 1.5).astype(jnp.bfloat16)


def draw_w_query(key, part):
    return weight_common(key, 1)


def draw_w_key(key, part):
    return weight_common(key, 2)


def draw_pair_list(key, part):
    key_list = jax.random.split(key, 2)
    hot_owner = jax.random.randint(key_list[0], (), 0, N_IMG).astype(jnp.int32)
    others = ((hot_owner + 1 + jnp.arange(N_IMG - 1, dtype=jnp.int32)) % N_IMG).astype(jnp.int32)
    owner_pool = jnp.tile(others, SLOT)

    def one_device(dev_key, device):
        key_perm, key_order, key_first, key_second = jax.random.split(dev_key, 4)
        picked = jax.random.permutation(key_perm, owner_pool)[:PAIR_DEV - SLOT]
        owners = jnp.concatenate([picked, jnp.full((SLOT,), hot_owner, jnp.int32)])
        owners = jax.random.permutation(key_order, owners)
        first_local = jax.random.randint(key_first, (PAIR_DEV,), 0, IMG_DEV).astype(jnp.int32)
        second_local = jax.random.randint(key_second, (PAIR_DEV,), 0, IMG_DEV).astype(jnp.int32)
        first_image = device * IMG_DEV + first_local
        second_image = owners * IMG_DEV + second_local
        moved = owners * IMG_DEV + (second_local + 1) % IMG_DEV
        second_image = jnp.where(second_image == first_image, moved, second_image)
        return jnp.stack([first_image, second_image], axis=1)
    pair_rows = jax.vmap(one_device)(jax.random.split(key_list[1], N_IMG), jnp.arange(N_IMG, dtype=jnp.int32))
    return pair_rows.reshape(PAIRS, 2).astype(jnp.int32)


def centred(stream_key, dims, scale, most, kind=jnp.bfloat16):
    entries = scale * jax.random.normal(stream_key, dims, jnp.float32)
    return jnp.clip(entries, min=-most, max=most).astype(kind)


def setup_inputs(seed: int = 0, part: int = 0) -> dict:
    keys = jax.random.split(jax.random.key(seed), 10)
    own_keys = jax.random.split(jax.random.fold_in(keys[9], part), 10)
    return {
        "tokens": draw_tokens(jax.random.fold_in(jax.random.fold_in(keys[9], part), 71), part),
        "pair_list": draw_pair_list(jax.random.fold_in(jax.random.fold_in(keys[9], part), 71), part),
        "w_query": draw_w_query(jax.random.fold_in(keys[9], 71), part),
        "w_key": draw_w_key(jax.random.fold_in(keys[9], 71), part),
        "w_value": centred(keys[4], (D, D), D ** -0.5, 0.21875),
        "w_out": centred(keys[5], (D, D), D ** -0.5, 0.21875),
        "gain_query": jnp.clip(1.0 + 0.18 * jax.random.normal(keys[6], (D,), jnp.float32), 0.1, 1.9),
        "context_norm_gain": jnp.clip(1.0 + 0.18 * jax.random.normal(keys[7], (D,), jnp.float32), 0.1, 1.9),
        "conf_weight": centred(keys[8], (D,), D ** -0.5, 0.21875, jnp.float32),
    }


EPSILON = 1e-06

def rounded(values):
    return lax.optimization_barrier(values.astype(jnp.bfloat16)).astype(jnp.float32)

def normalize(values, gain_vec):
    widened = values.astype(jnp.float32)
    centre = lax.optimization_barrier(jnp.mean(widened, axis=-1, keepdims=True))
    spread = lax.optimization_barrier(jnp.mean(jnp.square(widened - centre), axis=-1, keepdims=True))
    return ((widened - centre) * lax.rsqrt(spread + EPSILON) * gain_vec).astype(jnp.bfloat16)

def project(normed, weight):
    flat_rows = normed.reshape(-1, weight.shape[0])
    result = jnp.dot(flat_rows, weight, preferred_element_type=jnp.float32).astype(jnp.bfloat16)
    return result.reshape(normed.shape[:-1] + (weight.shape[1],))

def confidence(input_arrays, update, conf_weight):
    state_sum = input_arrays.astype(jnp.float32) + update.astype(jnp.float32)
    return 1.0 + jax.nn.softplus(lax.optimization_barrier(jnp.sum(state_sum * conf_weight, axis=-1)))

def branch(query_rows, key_rows, value_rows, w_out):
    head_dim = D // HEADS
    query_heads = query_rows.astype(jnp.float32).reshape(L, HEADS, head_dim)
    key_heads = key_rows.astype(jnp.float32).reshape(L, HEADS, head_dim)
    value_heads = value_rows.astype(jnp.float32).reshape(L, HEADS, head_dim)
    logit_scores = jnp.einsum('qhd,khd->hqk', query_heads, key_heads, precision=lax.Precision.HIGHEST) * (1.0 / math.sqrt(head_dim))
    row_max = lax.optimization_barrier(jnp.max(logit_scores, axis=-1, keepdims=True))
    exp_scores = jnp.exp(logit_scores - row_max)
    attn_probs = rounded(exp_scores / lax.optimization_barrier(jnp.sum(exp_scores, axis=-1, keepdims=True)))
    mixed = jnp.einsum('hqk,khd->qhd', attn_probs, value_heads, precision=lax.Precision.HIGHEST)
    mixed = mixed.reshape(L, D).astype(jnp.bfloat16)
    return jnp.dot(mixed, w_out, preferred_element_type=jnp.float32).astype(jnp.bfloat16)

def pick_row(source, index):
    return lax.dynamic_index_in_dim(source, index, 0, keepdims=False)

def reference(tokens, pair_list, w_query, w_key, w_value, w_out, gain_query, context_norm_gain, conf_weight):
    normed_query = normalize(tokens, gain_query)
    normed_context = normalize(tokens, context_norm_gain)
    all_queries = project(normed_query, w_query)
    all_keys = project(normed_context, w_key)
    all_values = project(normed_context, w_value)

    def one_pair(pair_row):
        first_id = pair_row[0]
        second_id = pair_row[1]
        update_one = branch(pick_row(all_queries, first_id), pick_row(all_keys, second_id), pick_row(all_values, second_id), w_out)
        update_two = branch(pick_row(all_queries, second_id), pick_row(all_keys, first_id), pick_row(all_values, first_id), w_out)
        conf_one = confidence(pick_row(tokens, first_id), update_one, conf_weight)
        conf_two = confidence(pick_row(tokens, second_id), update_two, conf_weight)
        return (conf_one[:, None] * update_one.astype(jnp.float32), conf_one, conf_two[:, None] * update_two.astype(jnp.float32), conf_two)
    weighted_one, conf_one, second_weighted, conf_two = lax.map(one_pair, pair_list)
    first_ids = pair_list[:, 0].astype(jnp.int32)
    second_ids = pair_list[:, 1].astype(jnp.int32)
    numerator = jax.ops.segment_sum(weighted_one, first_ids, num_segments=IMGS)
    numerator = numerator + jax.ops.segment_sum(second_weighted, second_ids, num_segments=IMGS)
    denominator = 1.0 + jax.ops.segment_sum(conf_one, first_ids, num_segments=IMGS)
    denominator = denominator + jax.ops.segment_sum(conf_two, second_ids, num_segments=IMGS)
    return tokens.astype(jnp.float32) + numerator / denominator[:, :, None]
```

```python
import functools
import math

import jax
import jax.numpy as jnp
from jax import lax
from jax.experimental import pallas as pl
from jax.experimental.pallas import tpu as pltpu
from jax.sharding import PartitionSpec as P

HEADS = 12
EPSILON = 1e-06
SLOTS = 2
PLANE = 4
VMEM = pl.BlockSpec(memory_space=pltpu.VMEM)
SMEM = pl.BlockSpec(memory_space=pltpu.SMEM)
ANY = pl.BlockSpec(memory_space=pl.ANY)
LIMIT = 56 * 1024 * 1024


def round_up(value, step):
    return (value + step - 1) // step * step


def image_at(ref, image, rows):
    if len(ref.shape) == 3:
        return ref.at[image]
    return ref.at[pl.ds(pl.multiple_of(image * rows, 8), rows)]


def centred_scaled(values):
    widened = values.astype(jnp.float32)
    centre = jnp.mean(widened, axis=-1, keepdims=True)
    shifted = widened - centre
    spread = jnp.mean(jnp.square(shifted), axis=-1, keepdims=True)
    return shifted * lax.rsqrt(spread + EPSILON)


def prep_kernel(tokens_ref, wq_t_ref, gain_ref, conf_row_ref, q_t_ref, conf_ref, normed):
    images, length, _ = tokens_ref.shape
    lanes = q_t_ref.shape[2]
    scale = 1.0 / math.sqrt(tokens_ref.shape[2] // HEADS)
    normed[...] = jnp.zeros_like(normed)
    diagonal = lax.broadcasted_iota(jnp.int32, (length, lanes), 0) == lax.broadcasted_iota(
        jnp.int32, (length, lanes), 1
    )

    def one_image(image, carry):
        own = tokens_ref[image]
        normed[0:length, :] = (centred_scaled(own) * gain_ref[...]).astype(jnp.bfloat16)
        queries = lax.dot_general(
            wq_t_ref[...],
            normed[...],
            (((1,), (1,)), ((), ())),
            preferred_element_type=jnp.float32,
        ).astype(jnp.bfloat16)
        q_t_ref[image] = queries * jnp.asarray(scale, jnp.bfloat16)
        sums = jnp.sum(own.astype(jnp.float32) * conf_row_ref[...], axis=-1, keepdims=True)
        conf_ref[image] = jnp.sum(jnp.where(diagonal, sums, 0.0), axis=0, keepdims=True)
        return carry

    lax.fori_loop(0, images, one_image, 0)


def image_is_needed(firsts_ref, seconds_ref, devices, asker, owner, slot):
    if slot == 0:
        spot = asker * devices + owner
        return seconds_ref[spot] - 1, firsts_ref[spot] - 1
    spot = owner * devices + asker
    return firsts_ref[spot] - 1, seconds_ref[spot] - 1


def branch_kernel(
    plan,
    devices,
    sources,
    first_call,
    last_call,
    firsts_ref,
    seconds_ref,
    me_ref,
    *refs,
):
    partner_refs = refs[:sources]
    rest = list(refs[sources:])
    tok_conf_ref, gain_ref, conf_col_ref = rest[:3]
    stored = rest[3:7]
    rest = rest[7:]
    if not first_call:
        denom_in, numer_in = rest[:2]
        rest = rest[2:]
    if last_call:
        tokens_in, merged_ref = rest[:2]
        numer, denom, tokens_ref = rest[2:5]
        rest = rest[5:]
    else:
        numer, denom = rest[:2]
        rest = rest[2:]
    q_t_ref, wk_ref, wv_t_ref, wo_t_ref = loaded = rest[:4]
    listed, whole_arrived, arrived, normed, keys, values_t, scores, probs, mixed_t = rest[4:13]
    copy_sem, load_sem = rest[13:]
    loads = [
        pltpu.make_async_copy(origin, target, load_sem.at[turn])
        for turn, (origin, target) in enumerate(zip(stored, loaded))
    ]
    if not first_call:
        loads.append(pltpu.make_async_copy(numer_in, numer, load_sem.at[4]))
    for turn in (1, 2, 0, 3, 4):
        if turn < len(loads):
            loads[turn].start()
    if last_call:
        tokens_load = pltpu.make_async_copy(tokens_in, tokens_ref, load_sem.at[5])
        tokens_load.start()
    images, feats, lanes = q_t_ref.shape
    length, rows = whole_arrived.shape[1], arrived.shape[1]
    key_rows = keys.shape[0]
    head_dim = feats // HEADS
    whole = length // 16 * 16
    me = me_ref[0]

    total = jnp.int32(0)
    for buffer_of, owner_of, slot, taken_of in plan:
        owner = owner_of(me)
        wanted, own = image_is_needed(firsts_ref, seconds_ref, devices, me, owner, slot)
        valid = (wanted >= 0) & taken_of(me)
        buffer, spot = buffer_of(me, wanted)

        @pl.when(valid)
        def _(total=total, buffer=buffer, spot=spot, own=own):
            listed[total, 0] = buffer
            listed[total, 1] = spot
            listed[total, 2] = own

        total = total + valid.astype(jnp.int32)

    def copies(turn, act):
        slot = turn % 2
        for source, ref in enumerate(partner_refs):

            @pl.when(listed[turn, 0] == source)
            def _(ref=ref):
                landing = whole_arrived if len(ref.shape) == 3 else arrived
                act(
                    pltpu.make_async_copy(
                        image_at(ref, listed[turn, 1], rows), landing.at[slot], copy_sem.at[slot]
                    )
                )
                if act is finish and len(ref.shape) == 3:
                    arrived[slot, 0:length, :] = whole_arrived[slot]

    def begin(copy):
        copy.start()

    def finish(copy):
        copy.wait()

    def fetch(turn):
        copies(turn, begin)

    @pl.when(total > 0)
    def _():
        fetch(0)

    normed[...] = jnp.zeros_like(normed)
    probs[:, key_rows:, :] = jnp.zeros((HEADS, lanes - key_rows, lanes), jnp.bfloat16)
    if first_call:
        numer[...] = jnp.zeros_like(numer)
        denom[...] = jnp.ones_like(denom)
    else:
        denom[...] = denom_in[...]

    tail_rows = lax.broadcasted_iota(jnp.int32, (key_rows - whole, 128), 0) + whole
    tail_ok = tail_rows < length

    def one_branch(turn, carry):
        slot = turn % 2
        copies(turn, finish)

        @pl.when(turn + 1 < total)
        def _():
            fetch(turn + 1)

        image = listed[turn, 2]

        def loaded_by_now(which):
            @pl.when(turn == 0)
            def _():
                loads[which].wait()

        normed[0:length, :] = (centred_scaled(arrived[slot, 0:length, :]) * gain_ref[...]).astype(jnp.bfloat16)
        loaded_by_now(1)
        keys[...] = jnp.dot(
            normed[0:key_rows, :], wk_ref[...], preferred_element_type=jnp.float32
        ).astype(jnp.bfloat16)
        loaded_by_now(2)
        values_t[...] = lax.dot_general(
            wv_t_ref[...],
            normed[...],
            (((1,), (1,)), ((), ())),
            preferred_element_type=jnp.float32,
        ).astype(jnp.bfloat16)
        zero_rows = jnp.zeros((head_dim, lanes), jnp.bfloat16)
        loaded_by_now(0)
        for head in range(HEADS):
            own_q = q_t_ref[image, head * head_dim : (head + 1) * head_dim, :]
            pair = head // 2
            ordered = [own_q, zero_rows] if head % 2 == 0 else [zero_rows, own_q]
            scores[head] = jnp.dot(
                keys[:, pair * 2 * head_dim : (pair + 1) * 2 * head_dim],
                jnp.concatenate(ordered, axis=0),
                preferred_element_type=jnp.float32,
            )
        for head in range(HEADS):
            for part in range(0, lanes, 128):
                body = scores[head, 0:whole, part : part + 128]
                tail = jnp.where(
                    tail_ok, scores[head, whole:key_rows, part : part + 128], -jnp.inf
                )
                top = jnp.maximum(
                    jnp.max(body, axis=0, keepdims=True), jnp.max(tail, axis=0, keepdims=True)
                )
                body = jnp.exp(body - top)
                tail = jnp.exp(tail - top)
                share = 1.0 / (
                    jnp.sum(body, axis=0, keepdims=True) + jnp.sum(tail, axis=0, keepdims=True)
                )
                probs[head, 0:whole, part : part + 128] = (body * share).astype(jnp.bfloat16)
                probs[head, whole:key_rows, part : part + 128] = (tail * share).astype(
                    jnp.bfloat16
                )
        for head in range(HEADS):
            part = slice(head * head_dim, (head + 1) * head_dim)
            mixed_t[part, :] = jnp.dot(
                values_t[part, :], probs[head], preferred_element_type=jnp.float32
            ).astype(jnp.bfloat16)
        loaded_by_now(3)
        update = (
            jnp.dot(wo_t_ref[...], mixed_t[...], preferred_element_type=jnp.float32)
            .astype(jnp.bfloat16)
            .astype(jnp.float32)
        )
        logit = tok_conf_ref[image] + jnp.concatenate(
            [
                jnp.sum(update[:, part : part + 128] * conf_col_ref[...], axis=0, keepdims=True)
                for part in range(0, lanes, 128)
            ],
            axis=1,
        )
        conf = 1.0 + jnp.maximum(logit, 0.0) + jnp.log1p(jnp.exp(-jnp.abs(logit)))
        if not first_call:
            loaded_by_now(4)
        numer[image] += conf * update
        denom[image] += conf
        return carry

    lax.fori_loop(0, total, one_branch, 0)

    @pl.when(total == 0)
    def _():
        for load in loads:
            load.wait()

    if last_call:
        tokens_load.wait()
        for image in range(images):
            ratio = jnp.transpose(numer[image] * (1.0 / denom[image]))
            merged = tokens_ref[image].astype(jnp.float32) + ratio[0:length, :]
            for part in range(feats // 128):
                merged_ref[
                    pl.ds(part * images + image, length, stride=feats // 128 * images), :
                ] = merged[:, part * 128 : (part + 1) * 128]


def pack_kernel(plan, devices, sources, firsts_ref, seconds_ref, me_ref, *refs):
    source_refs = refs[:sources]
    whole_staged, staged, in_sem, out_sem = refs[-4:]
    out_refs = refs[sources:-4]
    me = me_ref[0]
    length, rows = whole_staged.shape[1], staged.shape[1]
    jobs = []
    for spot, (buffer_of, owner_of, asker_of, slot, taken_of, out, place) in enumerate(plan):
        wanted, _ = image_is_needed(
            firsts_ref, seconds_ref, devices, asker_of(me), owner_of(me), slot
        )
        valid = (wanted >= 0) & taken_of(me)
        buffer, origin = buffer_of(me, wanted)
        for source, ref in enumerate(source_refs):
            landing = whole_staged if len(ref.shape) == 3 else staged
            jobs.append(
                (
                    spot,
                    valid & (buffer == source),
                    image_at(ref, origin, rows),
                    landing,
                    out_refs[out].at[pl.ds(place * rows, rows)],
                )
            )
    for spot, valid, origin, landing, _ in jobs:

        @pl.when(valid)
        def _(spot=spot, origin=origin, landing=landing):
            pltpu.make_async_copy(origin, landing.at[spot], in_sem.at[spot]).start()

    for spot, valid, origin, landing, target in jobs:

        @pl.when(valid)
        def _(spot=spot, origin=origin, landing=landing, target=target):
            pltpu.make_async_copy(origin, landing.at[spot], in_sem.at[spot]).wait()
            if landing is whole_staged:
                staged[spot, 0:length, :] = whole_staged[spot]
            pltpu.make_async_copy(staged.at[spot], target, out_sem.at[spot]).start()

    for spot, valid, _, _, target in jobs:

        @pl.when(valid)
        def _(spot=spot, target=target):
            pltpu.make_async_copy(staged.at[spot], target, out_sem.at[spot]).wait()


def pack(plan, tables, devices, length, sources, outs, places):
    rows, feats = round_up(length, 8), sources[0].shape[-1]
    return pl.pallas_call(
        functools.partial(pack_kernel, plan, devices, len(sources)),
        out_shape=tuple(
            jax.ShapeDtypeStruct((places * rows, feats), jnp.bfloat16) for _ in range(outs)
        ),
        in_specs=[SMEM] * 3 + [ANY] * len(sources),
        out_specs=(ANY,) * outs,
        scratch_shapes=[
            pltpu.VMEM((len(plan), length, feats), jnp.bfloat16),
            pltpu.VMEM((len(plan), rows, feats), jnp.bfloat16),
            pltpu.SemaphoreType.DMA((len(plan),)),
            pltpu.SemaphoreType.DMA((len(plan),)),
        ],
        compiler_params=pltpu.CompilerParams(vmem_limit_bytes=LIMIT),
        name="pack_images",
    )(*tables, *sources)


def run_branches(plan, tables, devices, length, partners, shared, sums, tokens=None):
    images, feats, lanes = shared[3].shape
    last_call = tokens is not None
    kept = (
        jax.ShapeDtypeStruct((images, feats, lanes), jnp.float32),
        jax.ShapeDtypeStruct((images, 1, lanes), jnp.float32),
    )
    operands = [*tables, *partners, *shared]
    specs = [SMEM] * 3 + [ANY] * len(partners) + [VMEM] * 3 + [ANY] * 4
    if sums is not None:
        operands += [sums[1], sums[0]]
        specs += [VMEM, ANY]
    scratch = []
    if last_call:
        operands.append(tokens)
        specs.append(ANY)
        outs = jax.ShapeDtypeStruct((length * images * feats // 128, 128), jnp.float32)
        out_specs = VMEM
        scratch = [pltpu.VMEM(k.shape, k.dtype) for k in (*kept, tokens)]
    else:
        outs, out_specs = kept, (VMEM, VMEM)
    key_rows = round_up(length, 16)
    scratch += [pltpu.VMEM(k.shape, k.dtype) for k in shared[3:]]
    scratch += [
        pltpu.SMEM((len(plan), 3), jnp.int32),
        pltpu.VMEM((2, length, feats), jnp.bfloat16),
        pltpu.VMEM((2, round_up(length, 8), feats), jnp.bfloat16),
        pltpu.VMEM((lanes, feats), jnp.bfloat16),
        pltpu.VMEM((key_rows, feats), jnp.bfloat16),
        pltpu.VMEM((feats, lanes), jnp.bfloat16),
        pltpu.VMEM((HEADS, key_rows, lanes), jnp.float32),
        pltpu.VMEM((HEADS, lanes, lanes), jnp.bfloat16),
        pltpu.VMEM((feats, lanes), jnp.bfloat16),
        pltpu.SemaphoreType.DMA((2,)),
        pltpu.SemaphoreType.DMA((6,)),
    ]
    expected = max(len(plan) // 2, 1)
    return pl.pallas_call(
        functools.partial(
            branch_kernel, plan, devices, len(partners), sums is None, last_call
        ),
        out_shape=outs,
        in_specs=specs,
        out_specs=out_specs,
        scratch_shapes=scratch,
        compiler_params=pltpu.CompilerParams(vmem_limit_bytes=LIMIT),
        cost_estimate=pl.CostEstimate(
            flops=expected * 1300000000, bytes_accessed=expected * 2000000, transcendentals=0
        ),
        name="attend_branches",
    )(*operands)


def prepare(tokens, wq_t, gain_query, conf_weight):
    images, length, feats = tokens.shape
    lanes = round_up(length, 128)
    return pl.pallas_call(
        prep_kernel,
        out_shape=(
            jax.ShapeDtypeStruct((images, feats, lanes), jnp.bfloat16),
            jax.ShapeDtypeStruct((images, 1, lanes), jnp.float32),
        ),
        in_specs=[VMEM] * 4,
        out_specs=(VMEM, VMEM),
        scratch_shapes=[pltpu.VMEM((lanes, feats), jnp.bfloat16)],
        compiler_params=pltpu.CompilerParams(vmem_limit_bytes=LIMIT),
        name="own_queries",
    )(tokens, wq_t, gain_query[None, :], conf_weight[None, :])


def pair_tables(pair_list, per_device, devices):
    pairs = lax.all_gather(pair_list, "img", axis=0, tiled=False)
    listing = jnp.arange(devices, dtype=jnp.int32)
    first_local = pairs[:, :, 0] - listing[:, None] * per_device
    owner = pairs[:, :, 1] // per_device
    second_local = pairs[:, :, 1] - owner * per_device
    hit = owner[:, :, None] == listing[None, None, :]
    firsts = jnp.sum(jnp.where(hit, first_local[:, :, None] + 1, 0), axis=1)
    seconds = jnp.sum(jnp.where(hit, second_local[:, :, None] + 1, 0), axis=1)
    return firsts, seconds


def always(me):
    return jnp.bool_(True)


def own_image(me, wanted):
    return 0, wanted


def fixed(buffer, spot):
    return lambda me, wanted: (buffer, spot)


def dense_exchange(tokens, tables, devices, shared):
    length = tokens.shape[1]
    places = [(other, slot) for other in range(devices) for slot in range(SLOTS)]
    packing = [
        (own_image, lambda me: me, lambda me, other=other: other, slot, always, 0, spot)
        for spot, (other, slot) in enumerate(places)
    ]
    (packed,) = pack(packing, tables, devices, length, (tokens,), 1, len(places))
    fetched = lax.all_to_all(packed, "img", split_axis=0, concat_axis=0, tiled=True)
    branches = [
        (fixed(0, spot), lambda me, other=other: other, slot, always)
        for spot, (other, slot) in enumerate(places)
    ]
    return run_branches(branches, tables, devices, length, (fetched,), shared, None, tokens)


def line_exchange(tokens, tables, devices, shared_of):
    length = tokens.shape[1]
    changes = range(1, PLANE)
    slots = range(SLOTS)
    pinned = lax.optimization_barrier

    def hop(array, step, origins):
        return lax.ppermute(
            array,
            "img",
            [(p * PLANE + c, (p + step) * PLANE + c) for p in origins for c in range(PLANE)],
        )

    def across(array, flip, change, planes=range(4)):
        return lax.ppermute(
            array,
            "img",
            [
                (p * PLANE + c, (p ^ flip) * PLANE + (c ^ change))
                for p in planes
                for c in range(PLANE)
            ],
        )

    def other(flip, change):
        return lambda me: ((me // PLANE) ^ flip) * PLANE + ((me % PLANE) ^ change)

    def same(me):
        return me

    def hopped(flip, base):
        return lambda me, wanted: (
            base + jnp.where((me // PLANE) ^ flip > me // PLANE, 1, 0),
            wanted,
        )

    def inner(me):
        plane = me // PLANE
        return (plane == 1) | (plane == 2)

    def outer(me):
        return jnp.logical_not(inner(me))

    def pack_for(packing, sources, outs):
        return pack(packing, tables, devices, length, sources, outs, SLOTS)

    def to_others(packed):
        return [across(packed[change - 1], 0, change) for change in changes]

    tokens, *tables = pinned((tokens, *tables))
    up_one = hop(tokens, 1, (0, 1, 2))
    down_one = hop(tokens, -1, (1, 2, 3))
    packing = [
        (own_image, same, other(0, change), slot, always, change - 1, slot)
        for change in changes
        for slot in slots
    ]
    within = to_others(pack_for(packing, (tokens,), PLANE - 1))
    shared = shared_of()
    up_one, down_one, within, shared = pinned((up_one, down_one, within, shared))

    up_two = hop(up_one, 1, (1, 2))
    down_two = hop(down_one, -1, (1, 2))
    packing = [
        entry
        for change in changes
        for slot in slots
        for entry in (
            (own_image, same, other(3, change), slot, outer, change - 1, slot),
            (hopped(3, 1), other(3, 0), other(0, change), slot, inner, change - 1, slot),
            (hopped(1, 1), other(1, 0), other(0, change), slot, always, change + PLANE - 2, slot),
        )
    ]
    packed = pack_for(packing, (tokens, up_one, down_one), 2 * (PLANE - 1))
    cross = to_others(packed[: PLANE - 1])
    shared, packed = pinned((shared, packed))
    branches = [
        (own_image if change == 0 else fixed(change, slot), other(0, change), slot, always)
        for change in range(PLANE)
        for slot in slots
    ]
    sums = run_branches(branches, tables, devices, length, (tokens, *within), shared, None)
    packed, cross, sums = pinned((packed, cross, sums))
    near = to_others(packed[PLANE - 1 :])
    packing = [
        (
            own_image if change == 0 else fixed(change, slot),
            other(0, change),
            other(3, 0),
            slot,
            outer,
            change // 2,
            change % 2 * SLOTS + slot,
        )
        for change in range(PLANE)
        for slot in slots
    ]
    ends = pack(packing, tables, devices, length, (tokens, *cross), 2, 2 * SLOTS)
    up_two, down_two, ends = pinned((up_two, down_two, ends))

    far = [across(part, 3, 0, (0, 3)) for part in ends]
    second = jnp.where(lax.axis_index("img") < 2 * PLANE, down_two, up_two)
    packing = [
        (own_image, other(2, 0), other(0, change), slot, always, change - 1, slot)
        for change in changes
        for slot in slots
    ]
    packed = pack_for(packing, (second,), PLANE - 1)
    packed, near = pinned((packed, near))
    third = to_others(packed)
    branches = [
        (
            hopped(1, 0) if change == 0 else fixed(1 + change, slot),
            other(1, change),
            slot,
            always,
        )
        for change in range(PLANE)
        for slot in slots
    ] + [
        (
            hopped(3, 0) if change == 0 else fixed(PLANE + change, slot),
            other(3, change),
            slot,
            inner,
        )
        for change in range(PLANE)
        for slot in slots
    ]
    sums = run_branches(
        branches, tables, devices, length, (up_one, down_one, *near, *cross), shared, sums
    )
    branches = [
        (own_image if change == 0 else fixed(change, slot), other(2, change), slot, always)
        for change in range(PLANE)
        for slot in slots
    ]
    sums = run_branches(branches, tables, devices, length, (second, *third), shared, sums)
    branches = [
        (fixed(change // 2, change % 2 * SLOTS + slot), other(3, change), slot, outer)
        for change in range(PLANE)
        for slot in slots
    ]
    return run_branches(branches, tables, devices, length, tuple(far), shared, sums, tokens)


def local(
    tokens, pair_list, w_query, w_key, w_value, w_out, gain_query, context_norm_gain, conf_weight
):
    per_device, length, feats = tokens.shape
    devices = lax.axis_size("img")
    me = lax.axis_index("img")
    firsts, seconds = pair_tables(pair_list, per_device, devices)
    tables = (firsts.reshape(-1), seconds.reshape(-1), me.astype(jnp.int32)[None])

    def shared_of():
        q_t, tok_conf = prepare(tokens, w_query.T, gain_query, conf_weight)
        return (
            tok_conf,
            context_norm_gain[None, :],
            jnp.broadcast_to(conf_weight[:, None], (feats, 128)),
            q_t,
            w_key,
            w_value.T,
            w_out.T,
        )

    if devices == 4 * PLANE:
        merged = line_exchange(tokens, tables, devices, shared_of)
    else:
        merged = dense_exchange(tokens, tables, devices, shared_of())
    merged = merged.reshape(length, feats // 128, per_device, 128)
    return jnp.transpose(merged, (2, 0, 1, 3)).reshape(per_device, length, feats)


def solution(mesh):
    return jax.shard_map(
        local,
        mesh=mesh,
        in_specs=(P(("groups", "img"), None, None), P(("groups", "img"), None)) + (P(),) * 7,
        out_specs=P(("groups", "img"), None, None),
        check_vma=False,
    )
```

```python
import functools
import math

import jax
import jax.numpy as jnp
from jax import lax
from jax.experimental import pallas as pl
from jax.experimental.pallas import tpu as pltpu
from jax.sharding import PartitionSpec as P

HEADS = 12
EPSILON = 1e-06
SLOTS = 2
PLANE = 4
VMEM = pl.BlockSpec(memory_space=pltpu.VMEM)
SMEM = pl.BlockSpec(memory_space=pltpu.SMEM)
ANY = pl.BlockSpec(memory_space=pl.ANY)
LIMIT = 56 * 1024 * 1024


def round_up(value, step):
    return (value + step - 1) // step * step


def image_at(ref, image, rows):
    if len(ref.shape) == 3:
        return ref.at[image]
    return ref.at[pl.ds(pl.multiple_of(image * rows, 8), rows)]


def centred_scaled(values):
    widened = values.astype(jnp.float32)
    centre = jnp.mean(widened, axis=-1, keepdims=True)
    shifted = widened - centre
    spread = jnp.mean(jnp.square(shifted), axis=-1, keepdims=True)
    return shifted * lax.rsqrt(spread + EPSILON)


def prep_kernel(tokens_ref, wq_t_ref, gain_ref, conf_row_ref, q_t_ref, conf_ref, normed):
    images, length, _ = tokens_ref.shape
    lanes = q_t_ref.shape[2]
    scale = 1.0 / math.sqrt(tokens_ref.shape[2] // HEADS)
    normed[...] = jnp.zeros_like(normed)
    diagonal = lax.broadcasted_iota(jnp.int32, (length, lanes), 0) == lax.broadcasted_iota(
        jnp.int32, (length, lanes), 1
    )

    def one_image(image, carry):
        own = tokens_ref[image]
        normed[0:length, :] = (centred_scaled(own) * gain_ref[...]).astype(jnp.bfloat16)
        queries = lax.dot_general(
            wq_t_ref[...],
            normed[...],
            (((1,), (1,)), ((), ())),
            preferred_element_type=jnp.float32,
        ).astype(jnp.bfloat16)
        q_t_ref[image] = queries * jnp.asarray(scale, jnp.bfloat16)
        sums = jnp.sum(own.astype(jnp.float32) * conf_row_ref[...], axis=-1, keepdims=True)
        conf_ref[image] = jnp.sum(jnp.where(diagonal, sums, 0.0), axis=0, keepdims=True)
        return carry

    lax.fori_loop(0, images, one_image, 0)


def image_is_needed(firsts_ref, seconds_ref, devices, asker, owner, slot):
    if slot == 0:
        spot = asker * devices + owner
        return seconds_ref[spot] - 1, firsts_ref[spot] - 1
    spot = owner * devices + asker
    return firsts_ref[spot] - 1, seconds_ref[spot] - 1


def branch_kernel(
    plan,
    devices,
    sources,
    first_call,
    last_call,
    firsts_ref,
    seconds_ref,
    me_ref,
    *refs,
):
    partner_refs = refs[:sources]
    rest = list(refs[sources:])
    tok_conf_ref, gain_ref, conf_col_ref = rest[:3]
    q_t_in = rest[3]
    stored = rest[4:7]
    rest = rest[7:]
    if not first_call:
        denom_in, numer_in = rest[:2]
        rest = rest[2:]
    if last_call:
        tokens_in, merged_ref = rest[:2]
        numer, denom, tokens_ref, earlier = rest[2:6]
        rest = rest[6:]
    else:
        numer, denom = rest[:2]
        rest = rest[2:]
    q_t_ref, wk_ref, wv_t_ref, wo_t_ref = rest[:4]
    listed, whole_arrived, arrived, normed, keys, values_t, scores, probs, mixed_t = rest[4:13]
    copy_sem, query_sem, load_sem = rest[13:]
    loads = [
        pltpu.make_async_copy(origin, target, load_sem.at[turn])
        for turn, (origin, target) in enumerate(zip(stored, rest[1:4]))
    ]
    late_loads = []
    if not first_call and not last_call:
        loads.append(pltpu.make_async_copy(numer_in, numer, load_sem.at[3]))
    if not first_call and last_call:
        late_loads.append(pltpu.make_async_copy(numer_in, earlier, load_sem.at[3]))
    if last_call:
        late_loads.append(pltpu.make_async_copy(tokens_in, tokens_ref, load_sem.at[4]))
    for load in loads + late_loads:
        load.start()
    images, feats, lanes = numer.shape
    length, rows = whole_arrived.shape[1], arrived.shape[1]
    key_rows = keys.shape[0]
    head_dim = feats // HEADS
    whole = length // 16 * 16
    me = me_ref[0]

    total = jnp.int32(0)
    for buffer_of, owner_of, slot, taken_of in plan:
        owner = owner_of(me)
        wanted, own = image_is_needed(firsts_ref, seconds_ref, devices, me, owner, slot)
        valid = (wanted >= 0) & taken_of(me)
        buffer, spot = buffer_of(me, wanted)

        @pl.when(valid)
        def _(total=total, buffer=buffer, spot=spot, own=own):
            listed[total, 0] = buffer
            listed[total, 1] = spot
            listed[total, 2] = own

        total = total + valid.astype(jnp.int32)

    def copies(turn, act):
        slot = turn % 2
        for source, ref in enumerate(partner_refs):

            @pl.when(listed[turn, 0] == source)
            def _(ref=ref):
                landing = whole_arrived if len(ref.shape) == 3 else arrived
                act(
                    pltpu.make_async_copy(
                        image_at(ref, listed[turn, 1], rows), landing.at[slot], copy_sem.at[slot]
                    )
                )
                if act is finish and len(ref.shape) == 3:
                    arrived[slot, 0:length, :] = whole_arrived[slot]

    def begin(copy):
        copy.start()

    def finish(copy):
        copy.wait()

    def queries_of(turn):
        slot = turn % 2
        return pltpu.make_async_copy(
            q_t_in.at[listed[turn, 2]], q_t_ref.at[slot], query_sem.at[slot]
        )

    def fetch(turn):
        copies(turn, begin)
        queries_of(turn).start()

    @pl.when(total > 0)
    def _():
        fetch(0)

    normed[...] = jnp.zeros_like(normed)
    probs[:, key_rows:, :] = jnp.zeros((HEADS, lanes - key_rows, lanes), jnp.bfloat16)
    if first_call or last_call:
        numer[...] = jnp.zeros_like(numer)
    denom[...] = jnp.ones_like(denom) if first_call else denom_in[...]

    tail_rows = lax.broadcasted_iota(jnp.int32, (key_rows - whole, 128), 0) + whole
    tail_ok = tail_rows < length

    def one_branch(turn, carry):
        slot = turn % 2
        copies(turn, finish)
        queries_of(turn).wait()

        @pl.when(turn + 1 < total)
        def _():
            fetch(turn + 1)

        image = listed[turn, 2]
        normed[0:length, :] = (centred_scaled(arrived[slot, 0:length, :]) * gain_ref[...]).astype(jnp.bfloat16)
        keys[...] = jnp.dot(
            normed[0:key_rows, :], wk_ref[...], preferred_element_type=jnp.float32
        ).astype(jnp.bfloat16)
        values_t[...] = lax.dot_general(
            wv_t_ref[...],
            normed[...],
            (((1,), (1,)), ((), ())),
            preferred_element_type=jnp.float32,
        ).astype(jnp.bfloat16)
        zero_rows = jnp.zeros((head_dim, lanes), jnp.bfloat16)
        for head in range(HEADS):
            own_q = q_t_ref[slot, head * head_dim : (head + 1) * head_dim, :]
            pair = head // 2
            ordered = [own_q, zero_rows] if head % 2 == 0 else [zero_rows, own_q]
            scores[head] = jnp.dot(
                keys[:, pair * 2 * head_dim : (pair + 1) * 2 * head_dim],
                jnp.concatenate(ordered, axis=0),
                preferred_element_type=jnp.float32,
            )
        for head in range(HEADS):
            for part in range(0, lanes, 128):
                body = scores[head, 0:whole, part : part + 128]
                tail = jnp.where(
                    tail_ok, scores[head, whole:key_rows, part : part + 128], -jnp.inf
                )
                top = jnp.maximum(
                    jnp.max(body, axis=0, keepdims=True), jnp.max(tail, axis=0, keepdims=True)
                )
                body = jnp.exp(body - top)
                tail = jnp.exp(tail - top)
                share = 1.0 / (
                    jnp.sum(body, axis=0, keepdims=True) + jnp.sum(tail, axis=0, keepdims=True)
                )
                probs[head, 0:whole, part : part + 128] = (body * share).astype(jnp.bfloat16)
                probs[head, whole:key_rows, part : part + 128] = (tail * share).astype(
                    jnp.bfloat16
                )
        for head in range(HEADS):
            part = slice(head * head_dim, (head + 1) * head_dim)
            mixed_t[part, :] = jnp.dot(
                values_t[part, :], probs[head], preferred_element_type=jnp.float32
            ).astype(jnp.bfloat16)
        update = (
            jnp.dot(wo_t_ref[...], mixed_t[...], preferred_element_type=jnp.float32)
            .astype(jnp.bfloat16)
            .astype(jnp.float32)
        )
        logit = tok_conf_ref[image] + jnp.concatenate(
            [
                jnp.sum(update[:, part : part + 128] * conf_col_ref[...], axis=0, keepdims=True)
                for part in range(0, lanes, 128)
            ],
            axis=1,
        )
        conf = 1.0 + jnp.maximum(logit, 0.0) + jnp.log1p(jnp.exp(-jnp.abs(logit)))
        numer[image] += conf * update
        denom[image] += conf
        return carry

    for load in loads:
        load.wait()
    lax.fori_loop(0, total, one_branch, 0)

    if last_call:
        for load in late_loads:
            load.wait()
        for image in range(images):
            total_numer = numer[image] if first_call else numer[image] + earlier[image]
            ratio = jnp.transpose(total_numer * (1.0 / denom[image]))
            merged = tokens_ref[image].astype(jnp.float32) + ratio[0:length, :]
            for part in range(feats // 128):
                merged_ref[
                    pl.ds(part * images + image, length, stride=feats // 128 * images), :
                ] = merged[:, part * 128 : (part + 1) * 128]


def pack_kernel(plan, devices, sources, firsts_ref, seconds_ref, me_ref, *refs):
    source_refs = refs[:sources]
    whole_staged, staged, in_sem, out_sem = refs[-4:]
    out_refs = refs[sources:-4]
    me = me_ref[0]
    length, rows = whole_staged.shape[1], staged.shape[1]
    jobs = []
    for spot, (buffer_of, owner_of, asker_of, slot, taken_of, out, place) in enumerate(plan):
        wanted, _ = image_is_needed(
            firsts_ref, seconds_ref, devices, asker_of(me), owner_of(me), slot
        )
        valid = (wanted >= 0) & taken_of(me)
        buffer, origin = buffer_of(me, wanted)
        for source, ref in enumerate(source_refs):
            landing = whole_staged if len(ref.shape) == 3 else staged
            jobs.append(
                (
                    spot,
                    valid & (buffer == source),
                    image_at(ref, origin, rows),
                    landing,
                    out_refs[out].at[pl.ds(place * rows, rows)],
                )
            )
    for spot, valid, origin, landing, _ in jobs:

        @pl.when(valid)
        def _(spot=spot, origin=origin, landing=landing):
            pltpu.make_async_copy(origin, landing.at[spot], in_sem.at[spot]).start()

    for spot, valid, origin, landing, target in jobs:

        @pl.when(valid)
        def _(spot=spot, origin=origin, landing=landing, target=target):
            pltpu.make_async_copy(origin, landing.at[spot], in_sem.at[spot]).wait()
            if landing is whole_staged:
                staged[spot, 0:length, :] = whole_staged[spot]
            pltpu.make_async_copy(staged.at[spot], target, out_sem.at[spot]).start()

    for spot, valid, _, _, target in jobs:

        @pl.when(valid)
        def _(spot=spot, target=target):
            pltpu.make_async_copy(staged.at[spot], target, out_sem.at[spot]).wait()


def pack(plan, tables, devices, length, sources, outs, places):
    rows, feats = round_up(length, 8), sources[0].shape[-1]
    return pl.pallas_call(
        functools.partial(pack_kernel, plan, devices, len(sources)),
        out_shape=tuple(
            jax.ShapeDtypeStruct((places * rows, feats), jnp.bfloat16) for _ in range(outs)
        ),
        in_specs=[SMEM] * 3 + [ANY] * len(sources),
        out_specs=(ANY,) * outs,
        scratch_shapes=[
            pltpu.VMEM((len(plan), length, feats), jnp.bfloat16),
            pltpu.VMEM((len(plan), rows, feats), jnp.bfloat16),
            pltpu.SemaphoreType.DMA((len(plan),)),
            pltpu.SemaphoreType.DMA((len(plan),)),
        ],
        compiler_params=pltpu.CompilerParams(vmem_limit_bytes=LIMIT),
        name="pack_images",
    )(*tables, *sources)


def run_branches(plan, tables, devices, length, partners, shared, sums, tokens=None):
    images, feats, lanes = shared[3].shape
    last_call = tokens is not None
    kept = (
        jax.ShapeDtypeStruct((images, feats, lanes), jnp.float32),
        jax.ShapeDtypeStruct((images, 1, lanes), jnp.float32),
    )
    operands = [*tables, *partners, *shared]
    specs = [SMEM] * 3 + [ANY] * len(partners) + [VMEM] * 3 + [ANY] * 4
    if sums is not None:
        operands += [sums[1], sums[0]]
        specs += [VMEM, ANY]
    scratch = []
    if last_call:
        operands.append(tokens)
        specs.append(ANY)
        outs = jax.ShapeDtypeStruct((length * images * feats // 128, 128), jnp.float32)
        out_specs = VMEM
        scratch = [pltpu.VMEM(k.shape, k.dtype) for k in (*kept, tokens)]
        scratch.append(pltpu.VMEM(kept[0].shape if sums is not None else (8, 128), jnp.float32))
    else:
        outs, out_specs = kept, (VMEM, VMEM)
    key_rows = round_up(length, 16)
    scratch.append(pltpu.VMEM((2, feats, lanes), jnp.bfloat16))
    scratch += [pltpu.VMEM(k.shape, k.dtype) for k in shared[4:]]
    scratch += [
        pltpu.SMEM((len(plan), 3), jnp.int32),
        pltpu.VMEM((2, length, feats), jnp.bfloat16),
        pltpu.VMEM((2, round_up(length, 8), feats), jnp.bfloat16),
        pltpu.VMEM((lanes, feats), jnp.bfloat16),
        pltpu.VMEM((key_rows, feats), jnp.bfloat16),
        pltpu.VMEM((feats, lanes), jnp.bfloat16),
        pltpu.VMEM((HEADS, key_rows, lanes), jnp.float32),
        pltpu.VMEM((HEADS, lanes, lanes), jnp.bfloat16),
        pltpu.VMEM((feats, lanes), jnp.bfloat16),
        pltpu.SemaphoreType.DMA((2,)),
        pltpu.SemaphoreType.DMA((2,)),
        pltpu.SemaphoreType.DMA((5,)),
    ]
    expected = max(len(plan) // 2, 1)
    return pl.pallas_call(
        functools.partial(
            branch_kernel, plan, devices, len(partners), sums is None, last_call
        ),
        out_shape=outs,
        in_specs=specs,
        out_specs=out_specs,
        scratch_shapes=scratch,
        compiler_params=pltpu.CompilerParams(vmem_limit_bytes=LIMIT),
        cost_estimate=pl.CostEstimate(
            flops=expected * 1300000000, bytes_accessed=expected * 2000000, transcendentals=0
        ),
        name="attend_branches",
    )(*operands)


def prepare(tokens, wq_t, gain_query, conf_weight):
    images, length, feats = tokens.shape
    lanes = round_up(length, 128)
    return pl.pallas_call(
        prep_kernel,
        out_shape=(
            jax.ShapeDtypeStruct((images, feats, lanes), jnp.bfloat16),
            jax.ShapeDtypeStruct((images, 1, lanes), jnp.float32),
        ),
        in_specs=[VMEM] * 4,
        out_specs=(VMEM, VMEM),
        scratch_shapes=[pltpu.VMEM((lanes, feats), jnp.bfloat16)],
        compiler_params=pltpu.CompilerParams(vmem_limit_bytes=LIMIT),
        name="own_queries",
    )(tokens, wq_t, gain_query[None, :], conf_weight[None, :])


def pair_tables(pair_list, per_device, devices):
    pairs = lax.all_to_all(
        jnp.broadcast_to(pair_list[None], (devices,) + pair_list.shape),
        "img",
        split_axis=0,
        concat_axis=0,
        tiled=True,
    )
    listing = jnp.arange(devices, dtype=jnp.int32)
    first_local = pairs[:, :, 0] - listing[:, None] * per_device
    owner = pairs[:, :, 1] // per_device
    second_local = pairs[:, :, 1] - owner * per_device
    hit = owner[:, :, None] == listing[None, None, :]
    firsts = jnp.sum(jnp.where(hit, first_local[:, :, None] + 1, 0), axis=1)
    seconds = jnp.sum(jnp.where(hit, second_local[:, :, None] + 1, 0), axis=1)
    return pairs, firsts, seconds


def always(me):
    return jnp.bool_(True)


def own_image(me, wanted):
    return 0, wanted


def fixed(buffer, spot):
    return lambda me, wanted: (buffer, spot)


def dense_exchange(tokens, tables, devices, shared):
    length = tokens.shape[1]
    places = [(other, slot) for other in range(devices) for slot in range(SLOTS)]
    packing = [
        (own_image, lambda me: me, lambda me, other=other: other, slot, always, 0, spot)
        for spot, (other, slot) in enumerate(places)
    ]
    (packed,) = pack(packing, tables, devices, length, (tokens,), 1, len(places))
    fetched = lax.all_to_all(packed, "img", split_axis=0, concat_axis=0, tiled=True)
    branches = [
        (fixed(0, spot), lambda me, other=other: other, slot, always)
        for spot, (other, slot) in enumerate(places)
    ]
    return run_branches(branches, tables, devices, length, (fetched,), shared, None, tokens)


def line_exchange(tokens, pairs, tables, devices, shared_of):
    length = tokens.shape[1]
    changes = range(1, PLANE)
    slots = range(SLOTS)
    pinned = lax.optimization_barrier

    def hop(array, step, origins):
        return lax.ppermute(
            array,
            "img",
            [(p * PLANE + c, (p + step) * PLANE + c) for p in origins for c in range(PLANE)],
        )

    def across(array, flip, change, planes=range(4)):
        return lax.ppermute(
            array,
            "img",
            [
                (p * PLANE + c, (p ^ flip) * PLANE + (c ^ change))
                for p in planes
                for c in range(PLANE)
            ],
        )

    def other(flip, change):
        return lambda me: ((me // PLANE) ^ flip) * PLANE + ((me % PLANE) ^ change)

    def same(me):
        return me

    def hopped(flip, base):
        return lambda me, wanted: (
            base + jnp.where((me // PLANE) ^ flip > me // PLANE, 1, 0),
            wanted,
        )

    def inner(me):
        plane = me // PLANE
        return (plane == 1) | (plane == 2)

    def outer(me):
        return jnp.logical_not(inner(me))

    def pack_for(packing, sources, outs):
        return pack(packing, tables, devices, length, sources, outs, SLOTS)

    def to_others(packed):
        return [across(packed[change - 1], 0, change) for change in changes]

    tokens, _ = pinned((tokens, pairs))
    up_one = hop(tokens, 1, (0, 1, 2))
    down_one = hop(tokens, -1, (1, 2, 3))
    packing = [
        (own_image, same, other(0, change), slot, always, change - 1, slot)
        for change in changes
        for slot in slots
    ]
    within = to_others(pack_for(packing, (tokens,), PLANE - 1))
    shared = shared_of()
    up_one, down_one, within, shared = pinned((up_one, down_one, within, shared))

    up_two = hop(up_one, 1, (1, 2))
    down_two = hop(down_one, -1, (1, 2))
    packing = [
        entry
        for change in changes
        for slot in slots
        for entry in (
            (own_image, same, other(3, change), slot, outer, change - 1, slot),
            (hopped(3, 1), other(3, 0), other(0, change), slot, inner, change - 1, slot),
            (hopped(1, 1), other(1, 0), other(0, change), slot, always, change + PLANE - 2, slot),
        )
    ]
    packed = pack_for(packing, (tokens, up_one, down_one), 2 * (PLANE - 1))
    cross = to_others(packed[: PLANE - 1])
    shared, packed = pinned((shared, packed))
    branches = [
        (own_image if change == 0 else fixed(change, slot), other(0, change), slot, always)
        for change in range(PLANE)
        for slot in slots
    ]
    sums = run_branches(branches, tables, devices, length, (tokens, *within), shared, None)
    packed, cross, sums = pinned((packed, cross, sums))
    near = to_others(packed[PLANE - 1 :])
    packing = [
        (
            own_image if change == 0 else fixed(change, slot),
            other(0, change),
            other(3, 0),
            slot,
            outer,
            change // 2,
            change % 2 * SLOTS + slot,
        )
        for change in range(PLANE)
        for slot in slots
    ]
    ends = pack(packing, tables, devices, length, (tokens, *cross), 2, 2 * SLOTS)
    up_two, down_two, ends = pinned((up_two, down_two, ends))

    far = [across(part, 3, 0, (0, 3)) for part in ends]
    second = jnp.where(lax.axis_index("img") < 2 * PLANE, down_two, up_two)
    packing = [
        (own_image, other(2, 0), other(0, change), slot, always, change - 1, slot)
        for change in changes
        for slot in slots
    ]
    packed = pack_for(packing, (second,), PLANE - 1)
    packed, near = pinned((packed, near))
    third = to_others(packed)
    branches = [
        (
            hopped(1, 0) if change == 0 else fixed(1 + change, slot),
            other(1, change),
            slot,
            always,
        )
        for change in range(PLANE)
        for slot in slots
    ] + [
        (
            hopped(3, 0) if change == 0 else fixed(PLANE + change, slot),
            other(3, change),
            slot,
            inner,
        )
        for change in range(PLANE)
        for slot in slots
    ]
    sums = run_branches(
        branches, tables, devices, length, (up_one, down_one, *near, *cross), shared, sums
    )
    branches = [
        (own_image if change == 0 else fixed(change, slot), other(2, change), slot, always)
        for change in range(PLANE)
        for slot in slots
    ]
    sums = run_branches(branches, tables, devices, length, (second, *third), shared, sums)
    branches = [
        (fixed(change // 2, change % 2 * SLOTS + slot), other(3, change), slot, outer)
        for change in range(PLANE)
        for slot in slots
    ]
    return run_branches(branches, tables, devices, length, tuple(far), shared, sums, tokens)


def local(
    tokens, pair_list, w_query, w_key, w_value, w_out, gain_query, context_norm_gain, conf_weight
):
    per_device, length, feats = tokens.shape
    devices = lax.axis_size("img")
    me = lax.axis_index("img")
    pairs, firsts, seconds = pair_tables(pair_list, per_device, devices)
    tables = (firsts.reshape(-1), seconds.reshape(-1), me.astype(jnp.int32)[None])

    def shared_of():
        q_t, tok_conf = prepare(tokens, w_query.T, gain_query, conf_weight)
        return (
            tok_conf,
            context_norm_gain[None, :],
            jnp.broadcast_to(conf_weight[:, None], (feats, 128)),
            q_t,
            w_key,
            w_value.T,
            w_out.T,
        )

    if devices == 4 * PLANE:
        merged = line_exchange(tokens, pairs, tables, devices, shared_of)
    else:
        merged = dense_exchange(tokens, tables, devices, shared_of())
    merged = merged.reshape(length, feats // 128, per_device, 128)
    return jnp.transpose(merged, (2, 0, 1, 3)).reshape(per_device, length, feats)


def solution(mesh):
    return jax.shard_map(
        local,
        mesh=mesh,
        in_specs=(P(("groups", "img"), None, None), P(("groups", "img"), None)) + (P(),) * 7,
        out_specs=P(("groups", "img"), None, None),
        check_vma=False,
    )
```

```python
import functools
import math

import jax
import jax.numpy as jnp
from jax import lax
from jax.experimental import pallas as pl
from jax.experimental.pallas import tpu as pltpu
from jax.sharding import PartitionSpec as P

HEADS = 12
EPSILON = 1e-06
SLOTS = 2
PLANE = 4
VMEM = pl.BlockSpec(memory_space=pltpu.VMEM)
SMEM = pl.BlockSpec(memory_space=pltpu.SMEM)
ANY = pl.BlockSpec(memory_space=pl.ANY)
HBM = pl.BlockSpec(memory_space=pltpu.HBM)
LIMIT = 50 * 1024 * 1024


def round_up(value, step):
    return (value + step - 1) // step * step


def image_at(ref, image, rows):
    if len(ref.shape) == 3:
        return ref.at[image]
    return ref.at[pl.ds(pl.multiple_of(image * rows, 8), rows)]


def centred_scaled(values):
    widened = values.astype(jnp.float32)
    centre = jnp.mean(widened, axis=-1, keepdims=True)
    shifted = widened - centre
    spread = jnp.mean(jnp.square(shifted), axis=-1, keepdims=True)
    return shifted * lax.rsqrt(spread + EPSILON)


def prep_kernel(tokens_ref, wq_t_ref, gain_ref, conf_row_ref, q_t_ref, conf_ref, normed):
    images, length, _ = tokens_ref.shape
    lanes = q_t_ref.shape[2]
    scale = 1.0 / math.sqrt(tokens_ref.shape[2] // HEADS)
    normed[...] = jnp.zeros_like(normed)
    diagonal = lax.broadcasted_iota(jnp.int32, (length, lanes), 0) == lax.broadcasted_iota(
        jnp.int32, (length, lanes), 1
    )

    def one_image(image, carry):
        own = tokens_ref[image]
        normed[0:length, :] = (centred_scaled(own) * gain_ref[...]).astype(jnp.bfloat16)
        queries = lax.dot_general(
            wq_t_ref[...],
            normed[...],
            (((1,), (1,)), ((), ())),
            preferred_element_type=jnp.float32,
        ).astype(jnp.bfloat16)
        q_t_ref[image] = queries * jnp.asarray(scale, jnp.bfloat16)
        sums = jnp.sum(own.astype(jnp.float32) * conf_row_ref[...], axis=-1, keepdims=True)
        conf_ref[image] = jnp.sum(jnp.where(diagonal, sums, 0.0), axis=0, keepdims=True)
        return carry

    lax.fori_loop(0, images, one_image, 0)


def image_is_needed(firsts_ref, seconds_ref, devices, asker, owner, slot):
    if slot == 0:
        spot = asker * devices + owner
        return seconds_ref[spot] - 1, firsts_ref[spot] - 1
    spot = owner * devices + asker
    return firsts_ref[spot] - 1, seconds_ref[spot] - 1


def branch_kernel(
    plan,
    devices,
    sources,
    parts,
    first_call,
    last_call,
    firsts_ref,
    seconds_ref,
    me_ref,
    *refs,
):
    partner_refs = refs[:sources]
    rest = list(refs[sources:])
    tok_conf_ref, gain_ref, conf_col_ref = rest[:3]
    q_t_in = rest[3]
    stored = rest[4:7]
    rest = rest[7:]
    denoms_in, numers_in = rest[:parts], rest[parts : 2 * parts]
    rest = rest[2 * parts :]
    if last_call:
        tokens_in, merged_ref = rest[:2]
        numer, denom, tokens_ref = rest[2:5]
        rest = rest[5:]
    else:
        numer_out, denom, numer = rest[:3]
        rest = rest[3:]
    earlier = rest[:parts]
    rest = rest[parts:]
    q_t_ref, wk_ref, wv_t_ref, wo_t_ref = rest[:4]
    listed, whole_arrived, arrived, normed, keys, values_t, scores, probs, mixed_t = rest[4:13]
    copy_sem, query_sem, load_sem, store_sem = rest[13:]
    loads = [
        pltpu.make_async_copy(origin, target, load_sem.at[turn])
        for turn, (origin, target) in enumerate(zip(stored, rest[1:4]))
    ]
    late_loads = [
        pltpu.make_async_copy(origin, target, load_sem.at[4 + turn])
        for turn, (origin, target) in enumerate(zip(numers_in, earlier))
    ]
    if last_call:
        late_loads.append(pltpu.make_async_copy(tokens_in, tokens_ref, load_sem.at[3]))
    for load in loads + late_loads:
        load.start()
    images, feats, lanes = numer.shape
    length, rows = whole_arrived.shape[1], arrived.shape[1]
    key_rows = keys.shape[0]
    head_dim = feats // HEADS
    whole = length // 16 * 16
    me = me_ref[0]

    total = jnp.int32(0)
    for buffer_of, owner_of, slot, taken_of in plan:
        owner = owner_of(me)
        wanted, own = image_is_needed(firsts_ref, seconds_ref, devices, me, owner, slot)
        valid = (wanted >= 0) & taken_of(me)
        buffer, spot = buffer_of(me, wanted)

        @pl.when(valid)
        def _(total=total, buffer=buffer, spot=spot, own=own):
            listed[total, 0] = buffer
            listed[total, 1] = spot
            listed[total, 2] = own

        total = total + valid.astype(jnp.int32)

    def copies(turn, act):
        slot = turn % 2
        for source, ref in enumerate(partner_refs):

            @pl.when(listed[turn, 0] == source)
            def _(ref=ref):
                landing = whole_arrived if len(ref.shape) == 3 else arrived
                act(
                    pltpu.make_async_copy(
                        image_at(ref, listed[turn, 1], rows), landing.at[slot], copy_sem.at[slot]
                    )
                )
                if act is finish and len(ref.shape) == 3:
                    arrived[slot, 0:length, :] = whole_arrived[slot]

    def begin(copy):
        copy.start()

    def finish(copy):
        copy.wait()

    def queries_of(turn):
        slot = turn % 2
        return pltpu.make_async_copy(
            q_t_in.at[listed[turn, 2]], q_t_ref.at[slot], query_sem.at[slot]
        )

    def fetch(turn):
        copies(turn, begin)
        queries_of(turn).start()

    @pl.when(total > 0)
    def _():
        fetch(0)

    normed[...] = jnp.zeros_like(normed)
    probs[:, key_rows:, :] = jnp.zeros((HEADS, lanes - key_rows, lanes), jnp.bfloat16)
    numer[...] = jnp.zeros_like(numer)
    denom[...] = jnp.ones_like(denom) if first_call else jnp.zeros_like(denom)
    for part in denoms_in:
        denom[...] += part[...]

    tail_rows = lax.broadcasted_iota(jnp.int32, (key_rows - whole, 128), 0) + whole
    tail_ok = tail_rows < length

    def one_branch(turn, carry):
        slot = turn % 2
        copies(turn, finish)
        queries_of(turn).wait()

        @pl.when(turn + 1 < total)
        def _():
            fetch(turn + 1)

        image = listed[turn, 2]
        normed[0:length, :] = (centred_scaled(arrived[slot, 0:length, :]) * gain_ref[...]).astype(jnp.bfloat16)
        keys[...] = jnp.dot(
            normed[0:key_rows, :], wk_ref[...], preferred_element_type=jnp.float32
        ).astype(jnp.bfloat16)
        values_t[...] = lax.dot_general(
            wv_t_ref[...],
            normed[...],
            (((1,), (1,)), ((), ())),
            preferred_element_type=jnp.float32,
        ).astype(jnp.bfloat16)
        zero_rows = jnp.zeros((head_dim, lanes), jnp.bfloat16)
        for head in range(HEADS):
            own_q = q_t_ref[slot, head * head_dim : (head + 1) * head_dim, :]
            pair = head // 2
            ordered = [own_q, zero_rows] if head % 2 == 0 else [zero_rows, own_q]
            scores[head] = jnp.dot(
                keys[:, pair * 2 * head_dim : (pair + 1) * 2 * head_dim],
                jnp.concatenate(ordered, axis=0),
                preferred_element_type=jnp.float32,
            )
        for head in range(HEADS):
            for part in range(0, lanes, 128):
                body = scores[head, 0:whole, part : part + 128]
                tail = jnp.where(
                    tail_ok, scores[head, whole:key_rows, part : part + 128], -jnp.inf
                )
                top = jnp.maximum(
                    jnp.max(body, axis=0, keepdims=True), jnp.max(tail, axis=0, keepdims=True)
                )
                body = jnp.exp(body - top)
                tail = jnp.exp(tail - top)
                share = 1.0 / (
                    jnp.sum(body, axis=0, keepdims=True) + jnp.sum(tail, axis=0, keepdims=True)
                )
                probs[head, 0:whole, part : part + 128] = (body * share).astype(jnp.bfloat16)
                probs[head, whole:key_rows, part : part + 128] = (tail * share).astype(
                    jnp.bfloat16
                )
        for head in range(HEADS):
            part = slice(head * head_dim, (head + 1) * head_dim)
            mixed_t[part, :] = jnp.dot(
                values_t[part, :], probs[head], preferred_element_type=jnp.float32
            ).astype(jnp.bfloat16)
        update = (
            jnp.dot(wo_t_ref[...], mixed_t[...], preferred_element_type=jnp.float32)
            .astype(jnp.bfloat16)
            .astype(jnp.float32)
        )
        logit = tok_conf_ref[image] + jnp.concatenate(
            [
                jnp.sum(update[:, part : part + 128] * conf_col_ref[...], axis=0, keepdims=True)
                for part in range(0, lanes, 128)
            ],
            axis=1,
        )
        conf = 1.0 + jnp.maximum(logit, 0.0) + jnp.log1p(jnp.exp(-jnp.abs(logit)))
        numer[image] += conf * update
        denom[image] += conf
        return carry

    for load in loads:
        load.wait()
    lax.fori_loop(0, total, one_branch, 0)

    for load in late_loads:
        load.wait()
    if not last_call:
        stores = []
        for image in range(images):
            if parts:
                numer[image] += functools.reduce(jnp.add, [part[image] for part in earlier])
            stores.append(
                pltpu.make_async_copy(
                    numer.at[image], numer_out.at[image], store_sem.at[image]
                )
            )
            stores[-1].start()
        for store in stores:
            store.wait()
    if last_call:
        for image in range(images):
            total_numer = functools.reduce(jnp.add, [part[image] for part in (numer, *earlier)])
            ratio = jnp.transpose(total_numer * (1.0 / denom[image]))
            merged = tokens_ref[image].astype(jnp.float32) + ratio[0:length, :]
            for part in range(feats // 128):
                merged_ref[
                    pl.ds(part * images + image, length, stride=feats // 128 * images), :
                ] = merged[:, part * 128 : (part + 1) * 128]


def pack_kernel(plan, devices, sources, firsts_ref, seconds_ref, me_ref, *refs):
    source_refs = refs[:sources]
    whole_staged, staged, in_sem, out_sem = refs[-4:]
    out_refs = refs[sources:-4]
    me = me_ref[0]
    length, rows = whole_staged.shape[1], staged.shape[1]
    jobs = []
    for spot, (buffer_of, owner_of, asker_of, slot, taken_of, out, place) in enumerate(plan):
        wanted, _ = image_is_needed(
            firsts_ref, seconds_ref, devices, asker_of(me), owner_of(me), slot
        )
        valid = (wanted >= 0) & taken_of(me)
        buffer, origin = buffer_of(me, wanted)
        for source, ref in enumerate(source_refs):
            landing = whole_staged if len(ref.shape) == 3 else staged
            jobs.append(
                (
                    spot,
                    valid & (buffer == source),
                    image_at(ref, origin, rows),
                    landing,
                    out_refs[out].at[pl.ds(place * rows, rows)],
                )
            )
    for spot, valid, origin, landing, _ in jobs:

        @pl.when(valid)
        def _(spot=spot, origin=origin, landing=landing):
            pltpu.make_async_copy(origin, landing.at[spot], in_sem.at[spot]).start()

    for spot, valid, origin, landing, target in jobs:

        @pl.when(valid)
        def _(spot=spot, origin=origin, landing=landing, target=target):
            pltpu.make_async_copy(origin, landing.at[spot], in_sem.at[spot]).wait()
            if landing is whole_staged:
                staged[spot, 0:length, :] = whole_staged[spot]
            pltpu.make_async_copy(staged.at[spot], target, out_sem.at[spot]).start()

    for spot, valid, _, _, target in jobs:

        @pl.when(valid)
        def _(spot=spot, target=target):
            pltpu.make_async_copy(staged.at[spot], target, out_sem.at[spot]).wait()


def pack(plan, tables, devices, length, sources, outs, places):
    rows, feats = round_up(length, 8), sources[0].shape[-1]
    staging = 2 * len(plan) * round_up(length, 16) * feats * 2
    return pl.pallas_call(
        functools.partial(pack_kernel, plan, devices, len(sources)),
        out_shape=tuple(
            jax.ShapeDtypeStruct((places * rows, feats), jnp.bfloat16) for _ in range(outs)
        ),
        in_specs=[SMEM] * 3 + [ANY] * len(sources),
        out_specs=(ANY,) * outs,
        scratch_shapes=[
            pltpu.VMEM((len(plan), length, feats), jnp.bfloat16),
            pltpu.VMEM((len(plan), rows, feats), jnp.bfloat16),
            pltpu.SemaphoreType.DMA((len(plan),)),
            pltpu.SemaphoreType.DMA((len(plan),)),
        ],
        compiler_params=pltpu.CompilerParams(vmem_limit_bytes=staging + 4 * 1024 * 1024),
        name="pack_images",
    )(*tables, *sources)


def run_branches(plan, tables, devices, length, partners, shared, first_call, sums, tokens=None):
    images, feats, lanes = shared[3].shape
    last_call = tokens is not None
    kept = (
        jax.ShapeDtypeStruct((images, feats, lanes), jnp.float32),
        jax.ShapeDtypeStruct((images, 1, lanes), jnp.float32),
    )
    operands = [*tables, *partners, *shared]
    specs = [SMEM] * 3 + [ANY] * len(partners) + [VMEM] * 3 + [ANY] * 4
    operands += [part[1] for part in sums] + [part[0] for part in sums]
    specs += [VMEM] * len(sums) + [HBM] * len(sums)
    scratch = []
    if last_call:
        operands.append(tokens)
        specs.append(ANY)
        outs = jax.ShapeDtypeStruct((length * images * feats // 128, 128), jnp.float32)
        out_specs = VMEM
        scratch = [pltpu.VMEM(k.shape, k.dtype) for k in (*kept, tokens)]
    else:
        outs, out_specs = kept, (HBM, VMEM)
        scratch = [pltpu.VMEM(kept[0].shape, jnp.float32)]
    key_rows = round_up(length, 16)
    scratch += [pltpu.VMEM(kept[0].shape, jnp.float32) for _ in sums]
    scratch.append(pltpu.VMEM((2, feats, lanes), jnp.bfloat16))
    scratch += [pltpu.VMEM(k.shape, k.dtype) for k in shared[4:]]
    scratch += [
        pltpu.SMEM((len(plan), 3), jnp.int32),
        pltpu.VMEM((2, length, feats), jnp.bfloat16),
        pltpu.VMEM((2, round_up(length, 8), feats), jnp.bfloat16),
        pltpu.VMEM((lanes, feats), jnp.bfloat16),
        pltpu.VMEM((key_rows, feats), jnp.bfloat16),
        pltpu.VMEM((feats, lanes), jnp.bfloat16),
        pltpu.VMEM((HEADS, key_rows, lanes), jnp.float32),
        pltpu.VMEM((HEADS, lanes, lanes), jnp.bfloat16),
        pltpu.VMEM((feats, lanes), jnp.bfloat16),
        pltpu.SemaphoreType.DMA((2,)),
        pltpu.SemaphoreType.DMA((2,)),
        pltpu.SemaphoreType.DMA((4 + len(sums),)),
        pltpu.SemaphoreType.DMA((images,)),
    ]
    expected = max(len(plan) // 2, 1)
    return pl.pallas_call(
        functools.partial(
            branch_kernel,
            plan,
            devices,
            len(partners),
            len(sums),
            first_call,
            last_call,
        ),
        out_shape=outs,
        in_specs=specs,
        out_specs=out_specs,
        scratch_shapes=scratch,
        compiler_params=pltpu.CompilerParams(vmem_limit_bytes=LIMIT),
        cost_estimate=pl.CostEstimate(
            flops=6 * 10**9, bytes_accessed=expected * 2000000, transcendentals=0
        ),
        name="attend_branches",
    )(*operands)


def prepare(tokens, wq_t, gain_query, conf_weight):
    images, length, feats = tokens.shape
    lanes = round_up(length, 128)
    return pl.pallas_call(
        prep_kernel,
        out_shape=(
            jax.ShapeDtypeStruct((images, feats, lanes), jnp.bfloat16),
            jax.ShapeDtypeStruct((images, 1, lanes), jnp.float32),
        ),
        in_specs=[VMEM] * 4,
        out_specs=(VMEM, VMEM),
        scratch_shapes=[pltpu.VMEM((lanes, feats), jnp.bfloat16)],
        compiler_params=pltpu.CompilerParams(vmem_limit_bytes=LIMIT),
        name="own_queries",
    )(tokens, wq_t, gain_query[None, :], conf_weight[None, :])


def pair_tables(pair_list, per_device, devices):
    pairs = lax.all_to_all(
        jnp.broadcast_to(pair_list[None], (devices,) + pair_list.shape),
        "img",
        split_axis=0,
        concat_axis=0,
        tiled=True,
    )
    listing = jnp.arange(devices, dtype=jnp.int32)
    first_local = pairs[:, :, 0] - listing[:, None] * per_device
    owner = pairs[:, :, 1] // per_device
    second_local = pairs[:, :, 1] - owner * per_device
    hit = owner[:, :, None] == listing[None, None, :]
    firsts = jnp.sum(jnp.where(hit, first_local[:, :, None] + 1, 0), axis=1)
    seconds = jnp.sum(jnp.where(hit, second_local[:, :, None] + 1, 0), axis=1)
    return pairs, firsts, seconds


def always(me):
    return jnp.bool_(True)


def own_image(me, wanted):
    return 0, wanted


def fixed(buffer, spot):
    return lambda me, wanted: (buffer, spot)


def dense_exchange(tokens, tables, devices, shared):
    length = tokens.shape[1]
    places = [(other, slot) for other in range(devices) for slot in range(SLOTS)]
    packing = [
        (own_image, lambda me: me, lambda me, other=other: other, slot, always, 0, spot)
        for spot, (other, slot) in enumerate(places)
    ]
    (packed,) = pack(packing, tables, devices, length, (tokens,), 1, len(places))
    fetched = lax.all_to_all(packed, "img", split_axis=0, concat_axis=0, tiled=True)
    branches = [
        (fixed(0, spot), lambda me, other=other: other, slot, always)
        for spot, (other, slot) in enumerate(places)
    ]
    return run_branches(branches, tables, devices, length, (fetched,), shared, True, (), tokens)


def line_exchange(tokens, pairs, tables, devices, shared_of):
    length = tokens.shape[1]
    changes = range(1, PLANE)
    slots = range(SLOTS)
    pinned = lax.optimization_barrier

    def hop(array, step, origins):
        return lax.ppermute(
            array,
            "img",
            [(p * PLANE + c, (p + step) * PLANE + c) for p in origins for c in range(PLANE)],
        )

    def across(array, flip, change, planes=range(4)):
        return lax.ppermute(
            array,
            "img",
            [
                (p * PLANE + c, (p ^ flip) * PLANE + (c ^ change))
                for p in planes
                for c in range(PLANE)
            ],
        )

    def other(flip, change):
        return lambda me: ((me // PLANE) ^ flip) * PLANE + ((me % PLANE) ^ change)

    def same(me):
        return me

    def hopped(flip, base):
        return lambda me, wanted: (
            base + jnp.where((me // PLANE) ^ flip > me // PLANE, 1, 0),
            wanted,
        )

    def inner(me):
        plane = me // PLANE
        return (plane == 1) | (plane == 2)

    def outer(me):
        return jnp.logical_not(inner(me))

    def pack_for(packing, sources, outs):
        return pack(packing, tables, devices, length, sources, outs, SLOTS)

    def to_others(packed):
        return [across(packed[change - 1], 0, change) for change in changes]

    tokens, _ = pinned((tokens, pairs))
    up_one = hop(tokens, 1, (0, 1, 2))
    down_one = hop(tokens, -1, (1, 2, 3))
    packing = [
        (own_image, same, other(0, change), slot, always, change - 1, slot)
        for change in changes
        for slot in slots
    ]
    within = to_others(pack_for(packing, (tokens,), PLANE - 1))
    shared = shared_of()
    up_one, down_one, within, shared = pinned((up_one, down_one, within, shared))

    up_two = hop(up_one, 1, (1, 2))
    down_two = hop(down_one, -1, (1, 2))
    packing = [
        entry
        for change in changes
        for slot in slots
        for entry in (
            (own_image, same, other(3, change), slot, outer, change - 1, slot),
            (hopped(3, 1), other(3, 0), other(0, change), slot, inner, change - 1, slot),
            (hopped(1, 1), other(1, 0), other(0, change), slot, always, change + PLANE - 2, slot),
        )
    ]
    packed = pack_for(packing, (tokens, up_one, down_one), 2 * (PLANE - 1))
    cross = to_others(packed[: PLANE - 1])
    shared, packed = pinned((shared, packed))
    branches = [
        (own_image if change == 0 else fixed(change, slot), other(0, change), slot, always)
        for change in range(PLANE)
        for slot in slots
    ]
    sums = run_branches(branches, tables, devices, length, (tokens, *within), shared, True, ())
    packed, cross, sums = pinned((packed, cross, sums))
    near = to_others(packed[PLANE - 1 :])
    packing = [
        (
            own_image if change == 0 else fixed(change, slot),
            other(0, change),
            other(3, 0),
            slot,
            outer,
            change // 2,
            change % 2 * SLOTS + slot,
        )
        for change in range(PLANE)
        for slot in slots
    ]
    ends = pack(packing, tables, devices, length, (tokens, *cross), 2, 2 * SLOTS)
    up_two, down_two, ends = pinned((up_two, down_two, ends))

    far_half = across(ends[0], 3, 0, (0, 3))
    second = jnp.where(lax.axis_index("img") < 2 * PLANE, down_two, up_two)
    packing = [
        (own_image, other(2, 0), other(0, change), slot, always, change - 1, slot)
        for change in changes
        for slot in slots
    ]
    packed = pack_for(packing, (second,), PLANE - 1)
    packed, near, end = pinned((packed, near, ends[1]))
    third = to_others(packed)
    last_half = across(end, 3, 0, (0, 3))
    branches = (
        [
            (
                hopped(1, 0) if change == 0 else fixed(1 + change, slot),
                other(1, change),
                slot,
                always,
            )
            for change in range(PLANE)
            for slot in slots
        ]
        + [
            (
                hopped(3, 0) if change == 0 else fixed(PLANE + change, slot),
                other(3, change),
                slot,
                inner,
            )
            for change in range(PLANE)
            for slot in slots
        ]
        + [
            (
                (lambda me, wanted: (2 * PLANE, wanted)) if change == 0 else fixed(2 * PLANE + 1, slot),
                other(2, change),
                slot,
                always,
            )
            for change in (0, 1)
            for slot in slots
        ]
    )
    more = run_branches(
        branches,
        tables,
        devices,
        length,
        (up_one, down_one, *near, *cross, second, third[0]),
        shared,
        False,
        (),
    )
    branches = [
        (fixed(change - 2, slot), other(2, change), slot, always)
        for change in (2, 3)
        for slot in slots
    ] + [
        (fixed(2, change * SLOTS + slot), other(3, change), slot, outer)
        for change in (0, 1)
        for slot in slots
    ]
    sums = run_branches(
        branches, tables, devices, length, (third[1], third[2], far_half), shared, False, (sums, more)
    )
    branches = [
        (fixed(0, (change - 2) * SLOTS + slot), other(3, change), slot, outer)
        for change in (2, 3)
        for slot in slots
    ]
    return run_branches(
        branches, tables, devices, length, (last_half,), shared, False, (sums,), tokens
    )


def local(
    tokens, pair_list, w_query, w_key, w_value, w_out, gain_query, context_norm_gain, conf_weight
):
    per_device, length, feats = tokens.shape
    devices = lax.axis_size("img")
    me = lax.axis_index("img")
    pairs, firsts, seconds = pair_tables(pair_list, per_device, devices)
    tables = (firsts.reshape(-1), seconds.reshape(-1), me.astype(jnp.int32)[None])

    def shared_of():
        q_t, tok_conf = prepare(tokens, w_query.T, gain_query, conf_weight)
        return (
            tok_conf,
            context_norm_gain[None, :],
            jnp.broadcast_to(conf_weight[:, None], (feats, 128)),
            q_t,
            w_key,
            w_value.T,
            w_out.T,
        )

    if devices == 4 * PLANE:
        merged = line_exchange(tokens, pairs, tables, devices, shared_of)
    else:
        merged = dense_exchange(tokens, tables, devices, shared_of())
    merged = merged.reshape(length, feats // 128, per_device, 128)
    return jnp.transpose(merged, (2, 0, 1, 3)).reshape(per_device, length, feats)


def solution(mesh):
    return jax.shard_map(
        local,
        mesh=mesh,
        in_specs=(P(("groups", "img"), None, None), P(("groups", "img"), None)) + (P(),) * 7,
        out_specs=P(("groups", "img"), None, None),
        check_vma=False,
    )
```

```python
import functools
import math

import jax
import jax.numpy as jnp
from jax import lax
from jax.experimental import pallas as pl
from jax.experimental.pallas import tpu as pltpu
from jax.sharding import PartitionSpec as P

HEADS = 12
EPSILON = 1e-06
SLOTS = 2
PLANE = 4
VMEM = pl.BlockSpec(memory_space=pltpu.VMEM)
SMEM = pl.BlockSpec(memory_space=pltpu.SMEM)
ANY = pl.BlockSpec(memory_space=pl.ANY)
HBM = pl.BlockSpec(memory_space=pltpu.HBM)
LIMIT = 50 * 1024 * 1024


def round_up(value, step):
    return (value + step - 1) // step * step


def image_at(ref, image, rows):
    if len(ref.shape) == 3:
        return ref.at[image]
    return ref.at[pl.ds(pl.multiple_of(image * rows, 8), rows)]


def centred_scaled(values):
    widened = values.astype(jnp.float32)
    centre = jnp.mean(widened, axis=-1, keepdims=True)
    shifted = widened - centre
    spread = jnp.mean(jnp.square(shifted), axis=-1, keepdims=True)
    return shifted * lax.rsqrt(spread + EPSILON)


def prep_kernel(tokens_ref, wq_t_ref, gain_ref, conf_row_ref, q_t_ref, conf_ref, normed):
    images, length, _ = tokens_ref.shape
    lanes = q_t_ref.shape[2]
    scale = 1.0 / math.sqrt(tokens_ref.shape[2] // HEADS)
    normed[...] = jnp.zeros_like(normed)
    diagonal = lax.broadcasted_iota(jnp.int32, (length, lanes), 0) == lax.broadcasted_iota(
        jnp.int32, (length, lanes), 1
    )

    def one_image(image, carry):
        own = tokens_ref[image]
        normed[0:length, :] = (centred_scaled(own) * gain_ref[...]).astype(jnp.bfloat16)
        queries = lax.dot_general(
            wq_t_ref[...],
            normed[...],
            (((1,), (1,)), ((), ())),
            preferred_element_type=jnp.float32,
        ).astype(jnp.bfloat16)
        q_t_ref[image] = queries * jnp.asarray(scale, jnp.bfloat16)
        sums = jnp.sum(own.astype(jnp.float32) * conf_row_ref[...], axis=-1, keepdims=True)
        conf_ref[image] = jnp.sum(jnp.where(diagonal, sums, 0.0), axis=0, keepdims=True)
        return carry

    lax.fori_loop(0, images, one_image, 0)


def image_is_needed(firsts_ref, seconds_ref, devices, asker, owner, slot):
    if slot == 0:
        spot = asker * devices + owner
        return seconds_ref[spot] - 1, firsts_ref[spot] - 1
    spot = owner * devices + asker
    return firsts_ref[spot] - 1, seconds_ref[spot] - 1


def branch_kernel(
    plan,
    devices,
    sources,
    parts,
    first_call,
    last_call,
    firsts_ref,
    seconds_ref,
    me_ref,
    *refs,
):
    partner_refs = refs[:sources]
    rest = list(refs[sources:])
    tok_conf_ref, gain_ref, conf_col_ref = rest[:3]
    q_t_in = rest[3]
    stored = rest[4:7]
    rest = rest[7:]
    denoms_in, numers_in = rest[:parts], rest[parts : 2 * parts]
    rest = rest[2 * parts :]
    if last_call:
        tokens_in, merged_ref = rest[:2]
        numer, denom, tokens_ref, merged_tiles = rest[2:6]
        rest = rest[6:]
    else:
        numer_out, denom, numer = rest[:3]
        rest = rest[3:]
    earlier = rest[:parts]
    rest = rest[parts:]
    q_t_ref, wk_ref, wv_t_ref, wo_t_ref = rest[:4]
    listed, whole_arrived, arrived, normed, keys, values_t, scores, probs, mixed_t = rest[4:13]
    copy_sem, query_sem, load_sem, store_sem = rest[13:]
    loads = [
        pltpu.make_async_copy(origin, target, load_sem.at[turn])
        for turn, (origin, target) in enumerate(zip(stored, rest[1:4]))
    ]
    late_loads = [
        pltpu.make_async_copy(origin, target, load_sem.at[4 + turn])
        for turn, (origin, target) in enumerate(zip(numers_in, earlier))
    ]
    if last_call:
        late_loads.append(pltpu.make_async_copy(tokens_in, tokens_ref, load_sem.at[3]))
    for load in loads + late_loads:
        load.start()
    images, feats, lanes = numer.shape
    length, rows = whole_arrived.shape[1], arrived.shape[1]
    key_rows = keys.shape[0]
    head_dim = feats // HEADS
    whole = length // 16 * 16
    me = me_ref[0]

    total = jnp.int32(0)
    for buffer_of, owner_of, slot, taken_of in plan:
        owner = owner_of(me)
        wanted, own = image_is_needed(firsts_ref, seconds_ref, devices, me, owner, slot)
        valid = (wanted >= 0) & taken_of(me)
        buffer, spot = buffer_of(me, wanted)

        @pl.when(valid)
        def _(total=total, buffer=buffer, spot=spot, own=own):
            listed[total, 0] = buffer
            listed[total, 1] = spot
            listed[total, 2] = own

        total = total + valid.astype(jnp.int32)

    whole_sources = sum(len(ref.shape) == 3 for ref in partner_refs)

    def copy_of(ref, turn):
        slot = turn % 2
        landing = whole_arrived if len(ref.shape) == 3 else arrived
        return pltpu.make_async_copy(
            image_at(ref, listed[turn, 1], rows), landing.at[slot], copy_sem.at[slot]
        )

    def finish(turn):
        slot = turn % 2
        if whole_sources:

            @pl.when(listed[turn, 0] < whole_sources)
            def _():
                copy_of(partner_refs[0], turn).wait()
                arrived[slot, 0:length, :] = whole_arrived[slot]

        if whole_sources < sources:

            @pl.when(listed[turn, 0] >= whole_sources)
            def _():
                copy_of(partner_refs[-1], turn).wait()

    def queries_of(turn):
        slot = turn % 2
        return pltpu.make_async_copy(
            q_t_in.at[listed[turn, 2]], q_t_ref.at[slot], query_sem.at[slot]
        )

    def fetch(turn):
        for source, ref in enumerate(partner_refs):

            @pl.when(listed[turn, 0] == source)
            def _(ref=ref):
                copy_of(ref, turn).start()

        queries_of(turn).start()

    @pl.when(total > 0)
    def _():
        fetch(0)

    normed[...] = jnp.zeros_like(normed)
    probs[:, key_rows:, :] = jnp.zeros((HEADS, lanes - key_rows, lanes), jnp.bfloat16)
    numer[...] = jnp.zeros_like(numer)
    denom[...] = jnp.ones_like(denom) if first_call else jnp.zeros_like(denom)
    for part in denoms_in:
        denom[...] += part[...]

    tail_rows = lax.broadcasted_iota(jnp.int32, (key_rows - whole, 128), 0) + whole
    tail_ok = tail_rows < length

    def one_branch(turn, carry):
        slot = turn % 2
        finish(turn)
        queries_of(turn).wait()

        @pl.when(turn + 1 < total)
        def _():
            fetch(turn + 1)

        image = listed[turn, 2]
        normed[0:length, :] = (centred_scaled(arrived[slot, 0:length, :]) * gain_ref[...]).astype(jnp.bfloat16)
        keys[...] = jnp.dot(
            normed[0:key_rows, :], wk_ref[...], preferred_element_type=jnp.float32
        ).astype(jnp.bfloat16)
        values_t[...] = lax.dot_general(
            wv_t_ref[...],
            normed[...],
            (((1,), (1,)), ((), ())),
            preferred_element_type=jnp.float32,
        ).astype(jnp.bfloat16)
        zero_rows = jnp.zeros((head_dim, lanes), jnp.bfloat16)
        for head in range(HEADS):
            own_q = q_t_ref[slot, head * head_dim : (head + 1) * head_dim, :]
            pair = head // 2
            ordered = [own_q, zero_rows] if head % 2 == 0 else [zero_rows, own_q]
            scores[head] = jnp.dot(
                keys[:, pair * 2 * head_dim : (pair + 1) * 2 * head_dim],
                jnp.concatenate(ordered, axis=0),
                preferred_element_type=jnp.float32,
            )
        for head in range(HEADS):
            for part in range(0, lanes, 128):
                body = scores[head, 0:whole, part : part + 128]
                tail = jnp.where(
                    tail_ok, scores[head, whole:key_rows, part : part + 128], -jnp.inf
                )
                top = jnp.maximum(
                    jnp.max(body, axis=0, keepdims=True), jnp.max(tail, axis=0, keepdims=True)
                )
                body = jnp.exp(body - top)
                tail = jnp.exp(tail - top)
                share = 1.0 / (
                    jnp.sum(body, axis=0, keepdims=True) + jnp.sum(tail, axis=0, keepdims=True)
                )
                probs[head, 0:whole, part : part + 128] = (body * share).astype(jnp.bfloat16)
                probs[head, whole:key_rows, part : part + 128] = (tail * share).astype(
                    jnp.bfloat16
                )
        for head in range(HEADS):
            part = slice(head * head_dim, (head + 1) * head_dim)
            mixed_t[part, :] = jnp.dot(
                values_t[part, :], probs[head], preferred_element_type=jnp.float32
            ).astype(jnp.bfloat16)
        update = (
            jnp.dot(wo_t_ref[...], mixed_t[...], preferred_element_type=jnp.float32)
            .astype(jnp.bfloat16)
            .astype(jnp.float32)
        )
        logit = tok_conf_ref[image] + jnp.concatenate(
            [
                jnp.sum(update[:, part : part + 128] * conf_col_ref[...], axis=0, keepdims=True)
                for part in range(0, lanes, 128)
            ],
            axis=1,
        )
        conf = 1.0 + jnp.maximum(logit, 0.0) + jnp.log1p(jnp.exp(-jnp.abs(logit)))
        numer[image] += conf * update
        denom[image] += conf
        return carry

    for load in loads:
        load.wait()
    lax.fori_loop(0, total, one_branch, 0)

    for load in late_loads:
        load.wait()
    if not last_call:
        stores = []
        for image in range(images):
            if parts:
                numer[image] += functools.reduce(jnp.add, [part[image] for part in earlier])
            stores.append(
                pltpu.make_async_copy(
                    numer.at[image], numer_out.at[image], store_sem.at[image]
                )
            )
            stores[-1].start()
        for store in stores:
            store.wait()
    if last_call:
        stores = []
        pieces = feats // 128
        for first in range(0, length, 128):
            count = min(128, length - first)
            for image in range(images):
                lane = slice(first, first + 128)
                ratio = functools.reduce(
                    jnp.add, [part[image, :, lane] for part in (numer, *earlier)]
                ) * (1.0 / denom[image, :, lane])
                own = tokens_ref[image, first : first + count, :].astype(jnp.float32)
                merged = own + jnp.transpose(ratio)[0:count, :]
                for piece in range(pieces):
                    merged_tiles[
                        pl.ds((first * pieces + piece) * images + image, count, stride=pieces * images), :
                    ] = merged[:, piece * 128 : (piece + 1) * 128]
            rows_done = pl.ds(first * pieces * images, count * pieces * images)
            stores.append(
                pltpu.make_async_copy(
                    merged_tiles.at[rows_done], merged_ref.at[rows_done], store_sem.at[first // 128]
                )
            )
            stores[-1].start()
        for store in stores:
            store.wait()


def pack_kernel(plan, devices, sources, firsts_ref, seconds_ref, me_ref, *refs):
    source_refs = refs[:sources]
    whole_staged, staged, in_sem, out_sem = refs[-4:]
    out_refs = refs[sources:-4]
    me = me_ref[0]
    length, rows = whole_staged.shape[1], staged.shape[1]
    jobs = []
    for spot, (buffer_of, owner_of, asker_of, slot, taken_of, out, place) in enumerate(plan):
        wanted, _ = image_is_needed(
            firsts_ref, seconds_ref, devices, asker_of(me), owner_of(me), slot
        )
        valid = (wanted >= 0) & taken_of(me)
        buffer, origin = buffer_of(me, wanted)
        for source, ref in enumerate(source_refs):
            landing = whole_staged if len(ref.shape) == 3 else staged
            jobs.append(
                (
                    spot,
                    valid & (buffer == source),
                    image_at(ref, origin, rows),
                    landing,
                    out_refs[out].at[pl.ds(place * rows, rows)],
                )
            )
    for spot, valid, origin, landing, _ in jobs:

        @pl.when(valid)
        def _(spot=spot, origin=origin, landing=landing):
            pltpu.make_async_copy(origin, landing.at[spot], in_sem.at[spot]).start()

    for spot, valid, origin, landing, target in jobs:

        @pl.when(valid)
        def _(spot=spot, origin=origin, landing=landing, target=target):
            pltpu.make_async_copy(origin, landing.at[spot], in_sem.at[spot]).wait()
            if landing is whole_staged:
                staged[spot, 0:length, :] = whole_staged[spot]
            pltpu.make_async_copy(staged.at[spot], target, out_sem.at[spot]).start()

    for spot, valid, _, _, target in jobs:

        @pl.when(valid)
        def _(spot=spot, target=target):
            pltpu.make_async_copy(staged.at[spot], target, out_sem.at[spot]).wait()


def pack(plan, tables, devices, length, sources, outs, places):
    rows, feats = round_up(length, 8), sources[0].shape[-1]
    staging = 2 * len(plan) * round_up(length, 16) * feats * 2
    return pl.pallas_call(
        functools.partial(pack_kernel, plan, devices, len(sources)),
        out_shape=tuple(
            jax.ShapeDtypeStruct((places * rows, feats), jnp.bfloat16) for _ in range(outs)
        ),
        in_specs=[SMEM] * 3 + [ANY] * len(sources),
        out_specs=(ANY,) * outs,
        scratch_shapes=[
            pltpu.VMEM((len(plan), length, feats), jnp.bfloat16),
            pltpu.VMEM((len(plan), rows, feats), jnp.bfloat16),
            pltpu.SemaphoreType.DMA((len(plan),)),
            pltpu.SemaphoreType.DMA((len(plan),)),
        ],
        compiler_params=pltpu.CompilerParams(vmem_limit_bytes=staging + 4 * 1024 * 1024),
        name="pack_images",
    )(*tables, *sources)


def run_branches(plan, tables, devices, length, partners, shared, first_call, sums, tokens=None):
    images, feats, lanes = shared[3].shape
    last_call = tokens is not None
    kept = (
        jax.ShapeDtypeStruct((images, feats, lanes), jnp.float32),
        jax.ShapeDtypeStruct((images, 1, lanes), jnp.float32),
    )
    operands = [*tables, *partners, *shared]
    specs = [SMEM] * 3 + [ANY] * len(partners) + [VMEM] * 3 + [ANY] * 4
    operands += [part[1] for part in sums] + [part[0] for part in sums]
    specs += [VMEM] * len(sums) + [HBM] * len(sums)
    scratch = []
    if last_call:
        operands.append(tokens)
        specs.append(ANY)
        outs = jax.ShapeDtypeStruct((length * images * feats // 128, 128), jnp.float32)
        out_specs = ANY
        scratch = [pltpu.VMEM(k.shape, k.dtype) for k in (*kept, tokens, outs)]
    else:
        outs, out_specs = kept, (HBM, VMEM)
        scratch = [pltpu.VMEM(kept[0].shape, jnp.float32)]
    key_rows = round_up(length, 16)
    scratch += [pltpu.VMEM(kept[0].shape, jnp.float32) for _ in sums]
    scratch.append(pltpu.VMEM((2, feats, lanes), jnp.bfloat16))
    scratch += [pltpu.VMEM(k.shape, k.dtype) for k in shared[4:]]
    scratch += [
        pltpu.SMEM((len(plan), 3), jnp.int32),
        pltpu.VMEM((2, length, feats), jnp.bfloat16),
        pltpu.VMEM((2, round_up(length, 8), feats), jnp.bfloat16),
        pltpu.VMEM((lanes, feats), jnp.bfloat16),
        pltpu.VMEM((key_rows, feats), jnp.bfloat16),
        pltpu.VMEM((feats, lanes), jnp.bfloat16),
        pltpu.VMEM((HEADS, key_rows, lanes), jnp.float32),
        pltpu.VMEM((HEADS, lanes, lanes), jnp.bfloat16),
        pltpu.VMEM((feats, lanes), jnp.bfloat16),
        pltpu.SemaphoreType.DMA((2,)),
        pltpu.SemaphoreType.DMA((2,)),
        pltpu.SemaphoreType.DMA((4 + len(sums),)),
        pltpu.SemaphoreType.DMA((images,)),
    ]
    expected = max(len(plan) // 2, 1)
    return pl.pallas_call(
        functools.partial(
            branch_kernel,
            plan,
            devices,
            len(partners),
            len(sums),
            first_call,
            last_call,
        ),
        out_shape=outs,
        in_specs=specs,
        out_specs=out_specs,
        scratch_shapes=scratch,
        compiler_params=pltpu.CompilerParams(vmem_limit_bytes=LIMIT),
        cost_estimate=pl.CostEstimate(
            flops=6 * 10**9, bytes_accessed=expected * 2000000, transcendentals=0
        ),
        name="attend_branches",
    )(*operands)


def prepare(tokens, wq_t, gain_query, conf_weight):
    images, length, feats = tokens.shape
    lanes = round_up(length, 128)
    return pl.pallas_call(
        prep_kernel,
        out_shape=(
            jax.ShapeDtypeStruct((images, feats, lanes), jnp.bfloat16),
            jax.ShapeDtypeStruct((images, 1, lanes), jnp.float32),
        ),
        in_specs=[VMEM] * 4,
        out_specs=(VMEM, VMEM),
        scratch_shapes=[pltpu.VMEM((lanes, feats), jnp.bfloat16)],
        compiler_params=pltpu.CompilerParams(vmem_limit_bytes=LIMIT),
        name="own_queries",
    )(tokens, wq_t, gain_query[None, :], conf_weight[None, :])


def pair_tables(pair_list, per_device, devices):
    pairs = lax.all_to_all(
        jnp.broadcast_to(pair_list[None], (devices,) + pair_list.shape),
        "img",
        split_axis=0,
        concat_axis=0,
        tiled=True,
    )
    listing = jnp.arange(devices, dtype=jnp.int32)
    first_local = pairs[:, :, 0] - listing[:, None] * per_device
    owner = pairs[:, :, 1] // per_device
    second_local = pairs[:, :, 1] - owner * per_device
    hit = owner[:, :, None] == listing[None, None, :]
    firsts = jnp.sum(jnp.where(hit, first_local[:, :, None] + 1, 0), axis=1)
    seconds = jnp.sum(jnp.where(hit, second_local[:, :, None] + 1, 0), axis=1)
    return pairs, firsts, seconds


def always(me):
    return jnp.bool_(True)


def own_image(me, wanted):
    return 0, wanted


def fixed(buffer, spot):
    return lambda me, wanted: (buffer, spot)


def dense_exchange(tokens, tables, devices, shared):
    length = tokens.shape[1]
    places = [(other, slot) for other in range(devices) for slot in range(SLOTS)]
    packing = [
        (own_image, lambda me: me, lambda me, other=other: other, slot, always, 0, spot)
        for spot, (other, slot) in enumerate(places)
    ]
    (packed,) = pack(packing, tables, devices, length, (tokens,), 1, len(places))
    fetched = lax.all_to_all(packed, "img", split_axis=0, concat_axis=0, tiled=True)
    branches = [
        (fixed(0, spot), lambda me, other=other: other, slot, always)
        for spot, (other, slot) in enumerate(places)
    ]
    return run_branches(branches, tables, devices, length, (fetched,), shared, True, (), tokens)


def line_exchange(tokens, pairs, tables, devices, shared_of):
    length = tokens.shape[1]
    changes = range(1, PLANE)
    slots = range(SLOTS)
    pinned = lax.optimization_barrier

    def hop(array, step, origins):
        return lax.ppermute(
            array,
            "img",
            [(p * PLANE + c, (p + step) * PLANE + c) for p in origins for c in range(PLANE)],
        )

    def across(array, flip, change, planes=range(4)):
        return lax.ppermute(
            array,
            "img",
            [
                (p * PLANE + c, (p ^ flip) * PLANE + (c ^ change))
                for p in planes
                for c in range(PLANE)
            ],
        )

    def other(flip, change):
        return lambda me: ((me // PLANE) ^ flip) * PLANE + ((me % PLANE) ^ change)

    def same(me):
        return me

    def hopped(flip, base):
        return lambda me, wanted: (
            base + jnp.where((me // PLANE) ^ flip > me // PLANE, 1, 0),
            wanted,
        )

    def inner(me):
        plane = me // PLANE
        return (plane == 1) | (plane == 2)

    def outer(me):
        return jnp.logical_not(inner(me))

    def pack_for(packing, sources, outs):
        return pack(packing, tables, devices, length, sources, outs, SLOTS)

    def to_others(packed):
        return [across(packed[change - 1], 0, change) for change in changes]

    tokens, _ = pinned((tokens, pairs))
    up_one = hop(tokens, 1, (0, 1, 2))
    down_one = hop(tokens, -1, (1, 2, 3))
    packing = [
        (own_image, same, other(0, change), slot, always, change - 1, slot)
        for change in changes
        for slot in slots
    ]
    within = to_others(pack_for(packing, (tokens,), PLANE - 1))
    shared = shared_of()
    up_one, down_one, within, shared = pinned((up_one, down_one, within, shared))

    up_two = hop(up_one, 1, (1, 2))
    down_two = hop(down_one, -1, (1, 2))
    packing = [
        entry
        for change in changes
        for slot in slots
        for entry in (
            (own_image, same, other(3, change), slot, outer, change - 1, slot),
            (hopped(3, 1), other(3, 0), other(0, change), slot, inner, change - 1, slot),
            (hopped(1, 1), other(1, 0), other(0, change), slot, always, change + PLANE - 2, slot),
        )
    ]
    packed = pack_for(packing, (tokens, up_one, down_one), 2 * (PLANE - 1))
    cross = to_others(packed[: PLANE - 1])
    shared, packed = pinned((shared, packed))
    branches = [
        (own_image if change == 0 else fixed(change, slot), other(0, change), slot, always)
        for change in range(PLANE)
        for slot in slots
    ]
    sums = run_branches(branches, tables, devices, length, (tokens, *within), shared, True, ())
    packed, cross, sums = pinned((packed, cross, sums))
    near = to_others(packed[PLANE - 1 :])
    packing = [
        (
            own_image if change == 0 else fixed(change, slot),
            other(0, change),
            other(3, 0),
            slot,
            outer,
            change // 2,
            change % 2 * SLOTS + slot,
        )
        for change in range(PLANE)
        for slot in slots
    ]
    ends = pack(packing, tables, devices, length, (tokens, *cross), 2, 2 * SLOTS)
    up_two, down_two, ends = pinned((up_two, down_two, ends))

    far_half = across(ends[0], 3, 0, (0, 3))
    second = jnp.where(lax.axis_index("img") < 2 * PLANE, down_two, up_two)
    packing = [
        (own_image, other(2, 0), other(0, change), slot, always, change - 1, slot)
        for change in changes
        for slot in slots
    ]
    packed = pack_for(packing, (second,), PLANE - 1)
    packed, near, end = pinned((packed, near, ends[1]))
    third = to_others(packed)
    last_half = across(end, 3, 0, (0, 3))
    branches = (
        [
            (
                hopped(1, 0) if change == 0 else fixed(2 + change, slot),
                other(1, change),
                slot,
                always,
            )
            for change in range(PLANE)
            for slot in slots
        ]
        + [
            (
                hopped(3, 0) if change == 0 else fixed(PLANE + 1 + change, slot),
                other(3, change),
                slot,
                inner,
            )
            for change in range(PLANE)
            for slot in slots
        ]
        + [
            (
                (lambda me, wanted: (2, wanted)) if change == 0 else fixed(2 * PLANE + 1, slot),
                other(2, change),
                slot,
                always,
            )
            for change in (0, 1)
            for slot in slots
        ]
    )
    more = run_branches(
        branches,
        tables,
        devices,
        length,
        (up_one, down_one, second, *near, *cross, third[0]),
        shared,
        False,
        (),
    )
    branches = [
        (fixed(change - 2, slot), other(2, change), slot, always)
        for change in (2, 3)
        for slot in slots
    ] + [
        (fixed(2, change * SLOTS + slot), other(3, change), slot, outer)
        for change in (0, 1)
        for slot in slots
    ]
    sums = run_branches(
        branches, tables, devices, length, (third[1], third[2], far_half), shared, False, (sums, more)
    )
    branches = [
        (fixed(0, (change - 2) * SLOTS + slot), other(3, change), slot, outer)
        for change in (2, 3)
        for slot in slots
    ]
    return run_branches(
        branches, tables, devices, length, (last_half,), shared, False, (sums,), tokens
    )


def local(
    tokens, pair_list, w_query, w_key, w_value, w_out, gain_query, context_norm_gain, conf_weight
):
    per_device, length, feats = tokens.shape
    devices = lax.axis_size("img")
    me = lax.axis_index("img")
    pairs, firsts, seconds = pair_tables(pair_list, per_device, devices)
    tables = (firsts.reshape(-1), seconds.reshape(-1), me.astype(jnp.int32)[None])

    def shared_of():
        q_t, tok_conf = prepare(tokens, w_query.T, gain_query, conf_weight)
        return (
            tok_conf,
            context_norm_gain[None, :],
            jnp.broadcast_to(conf_weight[:, None], (feats, 128)),
            q_t,
            w_key,
            w_value.T,
            w_out.T,
        )

    if devices == 4 * PLANE:
        merged = line_exchange(tokens, pairs, tables, devices, shared_of)
    else:
        merged = dense_exchange(tokens, tables, devices, shared_of())
    merged = merged.reshape(length, feats // 128, per_device, 128)
    return jnp.transpose(merged, (2, 0, 1, 3)).reshape(per_device, length, feats)


def solution(mesh):
    return jax.shard_map(
        local,
        mesh=mesh,
        in_specs=(P(("groups", "img"), None, None), P(("groups", "img"), None)) + (P(),) * 7,
        out_specs=P(("groups", "img"), None, None),
        check_vma=False,
    )
```
